512 devices in a mesh: ctx: 64 (over y, z), node: 4 (over x), tp: 2 (over core).
Axes of the slice: x: 4, y: 4, z: 16, core: 2. Of those that a mesh axis runs over, the one named last changes fastest.
Arguments:
- queries: bfloat16 [4, 8192, 1024], P('node', 'ctx', 'tp'), may hold values from -6 to 6
- key_vectors: bfloat16 [4, 8192, 1024], P('node', 'ctx', 'tp'), may hold values from -6 to 6
- value_vectors: bfloat16 [4, 8192, 2048], P('node', 'ctx', 'tp'), may hold values from -6 to 6
- decay_log: bfloat16 [4, 8192, 1024], P('node', 'ctx', 'tp'), may hold values from -16 to 0, as said below
- assignment: int32 [4, 64, 64], P('node'), may hold values from 0 to 4, as said below
- doc_lengths: int32 [8], replicated, may hold values from 1 to 24576, 32768 in all
- norm_gain: float32 [2048], P('tp'), may hold values from 0.5 to 1.5
Outputs:
- attended: bfloat16 [4, 8192, 2048], P('node', 'ctx', 'tp')
The draws below stay inside these ranges and needn't reach their ends.
Inputs may be any that keep to these rules, and one draw needn't show every extreme that they name: `assignment`: in each node group's 64 x 64 matrix every row and every column sums to 128; an entry of 4 occurs in every node group. `decay_log`: logarithms of positive rates.
All inputs are finite; a program needn't handle non-finite values.
Results may differ from the reference program's by a relative error of at most 0.001.
Values may be sent and summed in bfloat16 or wider, within the bound.
No kernel may reach another device: no remote copies, remote signals or barrier semaphores. Data moves between devices by JAX's collectives and lax.ppermute only.
A program may use at most 128 MiB of HBM per device.

```python
import math
import jax
import jax.numpy as jnp
import numpy as np
from jax import lax

HEADS = 8
DK = 128
DV = 256
TOK_DEV = 128
DOCS = 8
NODE_TOKENS = 8192
SEQ = 32768
N_CTX = 64
N_NODE = 4


def one_matrix(key):
    key_steps, key_shares, key_cols, key_rows = jax.random.split(key, 4)
    half = N_CTX // 2
    steps_drawn = jax.random.randint(key_steps, (half,), -2, 3)
    steps_drawn = steps_drawn.at[0].set(2)
    shares = jnp.concatenate([steps_drawn, -steps_drawn]) + TOK_DEV // N_CTX
    shares = jax.random.permutation(key_shares, shares)
    col_perm = jax.random.permutation(key_cols, N_CTX)
    row_perm = jax.random.permutation(key_rows, N_CTX)
    offsets = (col_perm[None, :] - row_perm[:, None]) % N_CTX
    return shares[offsets].astype(jnp.int32)


def draw_assignment(key, part):
    key = jax.random.fold_in(key, 5)
    node_keys = jax.random.split(key, N_NODE)
    return jax.vmap(one_matrix)(node_keys)


def draw_decay_log(key, part):
    key = jax.random.fold_in(key, 11)
    variety_random_key, gentle_random_key, quick_random_key, noise_random_key, spike_random_key, depth_random_key = jax.random.split(key, 6)
    channels = HEADS * DK
    sequence_total = N_NODE * NODE_TOKENS
    slow_share = 0.5
    slow_kind = jax.random.uniform(variety_random_key, (channels,)) < slow_share
    slow_rate = jnp.exp(jax.random.uniform(gentle_random_key, (channels,), jnp.float32, math.log(0.2 / sequence_total), math.log(2.0 / sequence_total)))
    fast_rate = jnp.exp(jax.random.uniform(quick_random_key, (channels,), jnp.float32, math.log(2.0 / sequence_total), math.log(1.0 / 30.0)))
    baseline_rate = jnp.where(slow_kind, slow_rate, fast_rate)
    noise_level = jnp.exp(jax.random.uniform(noise_random_key, (N_NODE, NODE_TOKENS, channels), jnp.float32, -0.7, 0.7))
    spike_rows = jax.random.uniform(spike_random_key, (N_NODE, NODE_TOKENS, 1)) < 8.0 / sequence_total
    spike_decay_rate = jax.random.uniform(depth_random_key, (N_NODE, NODE_TOKENS, 1), jnp.float32, 0.22, 0.69)
    decay_rate = baseline_rate[None, None, :] * noise_level + jnp.where(spike_rows, spike_decay_rate, 0.0)
    return jnp.log(decay_rate).astype(jnp.bfloat16)


def level_of(stream_key, dims, shards, smallest, high):
    def one(axis_at, shards_of):
        draws = jax.random.uniform(jax.random.fold_in(jax.random.fold_in(stream_key, 6), axis_at), (shards_of,), jnp.float32, smallest / len(shards), high / len(shards))
        return jnp.repeat(jnp.exp(draws), dims[axis_at] // shards_of).reshape((-1,) + (1,) * (len(dims) - axis_at - 1))

    level = one(*shards[0])
    for cut in shards[1:]:
        level = level * one(*cut)
    return level


def split_up(amount, total, limit, lean):
    loads = [(1 << 20) // math.isqrt(standing ** lean) + 1 for standing in range(2, amount + 1)]
    surplus, counts = total - limit - (amount - 1), [1] * (amount - 1)
    while surplus > 0:
        free = [i for i in range(amount - 1) if counts[i] < limit]
        mass, remaining = sum([loads[i] for i in free]), surplus
        for i in free:
            extra = min(limit - counts[i], max(1, remaining * loads[i] // mass), surplus)
            counts[i] = counts[i] + extra
            surplus = surplus - extra
    return np.array([limit] + counts)


def uneven(stream_key, number_of, total, bound, lean):
    if number_of == 2:
        one = jax.random.randint(stream_key, (), max(1, total - bound), min(bound, total - 1) + 1)
        return jnp.stack([one, total - one])
    lengths = jnp.asarray(split_up(number_of, total, bound, lean), jnp.int32)
    twos = (number_of - 1) // 2
    source_of, receiver = lengths[1:1 + 2 * twos:2], lengths[2:2 + 2 * twos:2]
    slack = jnp.minimum(source_of - 1, bound - receiver)
    passed = jax.random.randint(jax.random.fold_in(stream_key, 1), (twos,), 0, 1 << 20) % (slack + 1)
    lengths = lengths.at[1:1 + 2 * twos:2].set(source_of - passed).at[2:2 + 2 * twos:2].set(receiver + passed)
    return lengths[jax.random.permutation(jax.random.fold_in(stream_key, 2), number_of)]


def scatter_about(key, dims, scale, bound, cuts=(), kind=jnp.bfloat16):
    drawn = jax.random.normal(key, dims, jnp.float32) * scale
    if len(cuts) > 0:
        drawn = level_of(key, dims, cuts, -0.22, 0.18) * drawn
    return jnp.clip(drawn, min=-bound, max=bound).astype(kind)


def setup_inputs(seed: int = 0) -> dict:
    keys = jax.random.split(jax.random.key(seed), 8)
    queries = scatter_about(keys[0], (N_NODE, NODE_TOKENS, HEADS * DK), 1.0, 6.0, ((0, 4), (1, 64), (2, 2)))
    key_vectors = scatter_about(keys[1], (N_NODE, NODE_TOKENS, HEADS * DK), 1.0, 6.0, ((0, 4), (1, 64), (2, 2)))
    value_vectors = scatter_about(keys[2], (N_NODE, NODE_TOKENS, HEADS * DV), 1.0, 6.0, ((0, 4), (1, 64), (2, 2)))
    decay_log = draw_decay_log(jax.random.fold_in(keys[7], 71), 0)
    assignment = draw_assignment(jax.random.fold_in(keys[7], 71), 0)
    doc_lengths = uneven(keys[5], DOCS, SEQ, SEQ * 3 // 4, 2).astype(jnp.int32)
    norm_gain = jnp.clip(1.0 + 0.1 * jax.random.normal(keys[6], (HEADS * DV,), jnp.float32), 0.5, 1.5)
    return {"queries": queries, "key_vectors": key_vectors, "value_vectors": value_vectors, "decay_log": decay_log, "assignment": assignment, "doc_lengths": doc_lengths, "norm_gain": norm_gain}


PRECISE = lax.Precision.HIGHEST
EPSILON = 1e-05

def regroup_node(loader_rows, matrix):
    src_incl = jnp.cumsum(matrix, axis=1).astype(jnp.int32)
    src_start = (src_incl - matrix).astype(jnp.int32)
    dst_start = (jnp.cumsum(matrix, axis=0) - matrix).astype(jnp.int32)
    within = jnp.arange(TOK_DEV, dtype=jnp.int32)
    owner = lax.optimization_barrier(jnp.sum((src_incl[:, None, :] <= within[None, :, None]).astype(jnp.int32), axis=2)).astype(jnp.int32)
    src_at = jnp.take_along_axis(src_start, owner, axis=1)
    dst_at = jnp.take_along_axis(dst_start, owner, axis=1)
    target = (owner * TOK_DEV + dst_at + within[None, :] - src_at).reshape(-1).astype(jnp.int32)
    return jnp.zeros_like(loader_rows).at[target].set(loader_rows)

def block_step(query_f, key_f, value_f, rate_log, doc_ids, doc_before, carry_state):
    log_decay = -jnp.exp(rate_log)
    cumulative = jnp.cumsum(log_decay, axis=0)
    dec_query = query_f * jnp.exp(cumulative)
    inv_key = key_f * jnp.exp(-cumulative)
    scores = jnp.einsum('thc,shc->hts', dec_query, inv_key, precision=PRECISE)
    places = jnp.arange(doc_ids.shape[0], dtype=jnp.int32)
    allowed = (places[:, None] >= places[None, :]) & (doc_ids[:, None] == doc_ids[None, :])
    scores = jnp.where(allowed[None], scores, 0.0)
    local_out = jnp.einsum('hts,shv->htv', scores, value_f, precision=PRECISE)
    keep_mask = (doc_ids == doc_before).astype(jnp.float32)
    carried = jnp.einsum('thc,hcv->htv', dec_query, carry_state, precision=PRECISE) * keep_mask[None, :, None]
    last_doc = (doc_ids == doc_ids[-1]).astype(jnp.float32)
    end_key = key_f * jnp.exp(cumulative[-1][None] - cumulative) * last_doc[:, None, None]
    fresh_state = jnp.einsum('shc,shv->hcv', end_key, value_f, precision=PRECISE)
    multiplier = jnp.exp(cumulative[-1]) * (doc_ids[-1] == doc_before).astype(jnp.float32)
    new_state = multiplier[:, :, None] * carry_state + fresh_state
    return (local_out + carried, new_state)

def reference(queries, key_vectors, value_vectors, decay_log, assignment, doc_lengths, norm_gain):
    total = N_NODE * NODE_TOKENS
    blocks = total // TOK_DEV
    streams = []
    for stream, width in ((queries, DK), (key_vectors, DK), (value_vectors, DV), (decay_log, DK)):
        ordered = jax.vmap(regroup_node)(stream, assignment)
        streams.append(ordered.reshape(blocks, TOK_DEV, HEADS, width))
    ends = jnp.cumsum(doc_lengths).astype(jnp.int32)
    places = jnp.arange(total, dtype=jnp.int32)
    doc_all = lax.optimization_barrier(jnp.sum((ends[None, :] <= places[:, None]).astype(jnp.int32), axis=1)).astype(jnp.int32)
    doc_ids = doc_all.reshape(blocks, TOK_DEV)
    doc_before = jnp.concatenate([jnp.zeros((1,), jnp.int32), doc_ids[:-1, -1]]).astype(jnp.int32)
    gains = norm_gain.reshape(HEADS, DV)

    def step(carry_state, inputs):
        query_b, key_b, value_b, rate_b, doc_b, before_b = inputs
        mixed, new_state = block_step(query_b.astype(jnp.float32), key_b.astype(jnp.float32), value_b.astype(jnp.float32), rate_b.astype(jnp.float32), doc_b, before_b, carry_state)
        scale = lax.rsqrt(lax.optimization_barrier(jnp.mean(mixed * mixed, axis=2, keepdims=True)) + EPSILON)
        normed = mixed * scale * gains[:, None, :]
        return (new_state, jnp.transpose(normed, (1, 0, 2)).astype(jnp.bfloat16))
    initial = jnp.zeros((HEADS, DK, DV), jnp.float32)
    _, outputs = lax.scan(step, initial, (streams[0], streams[1], streams[2], streams[3], doc_ids, doc_before))
    return outputs.reshape(N_NODE, NODE_TOKENS, HEADS * DV)
```

```python
import functools

import jax
import jax.numpy as jnp
from jax import lax
from jax.experimental import pallas as pl
from jax.experimental.pallas import tpu as pltpu
from jax.sharding import Mesh, PartitionSpec as P

DK = 128
DV = 256
HEADS = 4
GROUP = 4
TOK = 128
CAP = 16
CHUNK = GROUP * TOK
OWNERS = 64
WIDTH = 3 * DK + DV
EPSILON = 1e-05
CTX = ("y", "zh", "zl")
CHUNKS = ("node", "y", "zh")
PRECISE = lax.Precision.HIGHEST
F32 = jnp.float32
BF16 = jnp.bfloat16


def iota(shape, dim):
    return lax.broadcasted_iota(jnp.int32, shape, dim)


def dot(a, b, dims=((1,), (0,)), precision=None):
    return lax.dot_general(a, b, (dims, ((), ())), precision=precision, preferred_element_type=F32)


def pack_kernel(place_ref, matrix_ref, query_ref, key_ref, value_ref, rate_ref, out_ref):
    slots = (OWNERS // GROUP) * CAP
    counts = matrix_ref[pl.ds(place_ref[0], 1), :].astype(F32)
    chunk = lax.shift_right_logical(iota((slots, OWNERS), 0), 4)
    before = iota((slots, OWNERS), 1) < chunk * GROUP
    start = jnp.sum(jnp.where(before, counts, 0.0), axis=1, keepdims=True).astype(jnp.int32)
    wanted = start + (iota((slots, 1), 0) & (CAP - 1))
    pick = (iota((slots, TOK), 1) == wanted).astype(F32).astype(BF16)
    at = 0
    for ref, width in ((query_ref, DK), (key_ref, DK), (value_ref, DV), (rate_ref, DK)):
        rows = dot(pick, ref[...]).astype(BF16)
        for head in range(HEADS):
            piece = rows[:, head * width : (head + 1) * width]
            out_ref[:, head, :, at : at + width] = piece.reshape(slots // CAP, CAP, width)
        at += width


def doc_of(lengths_ref, places):
    end = jnp.int32(0)
    doc = jnp.zeros_like(places)
    for d in range(lengths_ref.shape[0]):
        end = end + lengths_ref[d]
        doc = doc + (end <= places).astype(jnp.int32)
    return doc


def unpack(place_ref, matrix_ref, received_ref):
    first = place_ref[1] * GROUP
    matrix = matrix_ref[...].astype(F32).astype(BF16)
    owner = iota((8, OWNERS), 1)
    nth = iota((8, OWNERS), 0)
    one = ((owner == first + nth) & (nth < GROUP)).astype(F32).astype(BF16)
    upto = ((owner >= first) & (owner <= first + nth) & (nth < GROUP)).astype(F32).astype(BF16)
    counts = dot(one, matrix, ((1,), (1,)))
    ends = dot(upto, matrix, ((1,), (1,)))
    earlier = (iota((OWNERS, OWNERS), 0) < iota((OWNERS, OWNERS), 1)).astype(F32).astype(BF16)
    arrive = dot(counts.astype(BF16), earlier)
    slots = OWNERS * CAP
    expand = (lax.shift_right_logical(iota((OWNERS, slots), 1), 4) == iota((OWNERS, slots), 0)).astype(F32).astype(BF16)
    counts, ends, arrive = [dot(a.astype(BF16), expand) for a in (counts, ends, arrive)]
    slot = (iota((8, slots), 1) & (CAP - 1)).astype(F32)
    inside = (slot < ends) & (slot >= ends - counts)
    target = iota((8, slots), 0).astype(F32) * TOK + arrive + slot - (ends - counts) + 1.0
    target = jnp.sum(jnp.where(inside, target, 0.0), axis=0, keepdims=True).astype(jnp.int32) - 1
    pick = (iota((CHUNK, slots), 0) == target).astype(F32).astype(BF16)
    return dot(pick, received_ref[...].reshape(slots, WIDTH))


def column(row):
    return jnp.transpose(jnp.broadcast_to(row, (DK, DK)))


def chunk_kernel(
    place_ref, lengths_ref, matrix_ref, received_ref, map_ref, partial_ref, query_out_ref
):
    rows = unpack(place_ref, matrix_ref, received_ref)
    first = (place_ref[2] * (OWNERS // GROUP) + place_ref[1]) * CHUNK
    tril = (iota((TOK, TOK), 0) >= iota((TOK, TOK), 1)).astype(F32)
    state = None
    passed = jnp.zeros((1, DK), F32)
    chunk_before = doc_of(lengths_ref, jnp.full((1, 1), first - 1, jnp.int32))
    for block in range(GROUP):
        here = rows[block * TOK : (block + 1) * TOK]
        query, key = here[:, :DK], here[:, DK : 2 * DK]
        value, rate = here[:, 2 * DK : 2 * DK + DV], here[:, 2 * DK + DV :]
        start = first + block * TOK
        doc_rows = doc_of(lengths_ref, start + iota((TOK, DK), 0))
        doc_columns = doc_of(lengths_ref, start + iota((TOK, TOK), 1))
        doc_before = doc_of(lengths_ref, jnp.full((1, 1), start - 1, jnp.int32))
        doc_last = doc_of(lengths_ref, jnp.full((1, 1), start + TOK - 1, jnp.int32))
        cumulative = dot(tril, -jnp.exp(rate), precision=PRECISE)
        whole = cumulative[TOK - 1 :, :]
        half = 0.5 * whole
        scores = dot(
            query * jnp.exp(cumulative - half),
            key * jnp.exp(half - cumulative),
            ((1,), (1,)),
            PRECISE,
        )
        allowed = (iota((TOK, TOK), 0) >= iota((TOK, TOK), 1)) & (doc_rows == doc_columns)
        out = dot(jnp.where(allowed, scores, 0.0), value, precision=PRECISE)
        if block > 0:
            kept = jnp.where(doc_rows == doc_before, query * jnp.exp(cumulative), 0.0)
            out = out + dot(kept, state, precision=PRECISE)
        span = slice(block * TOK, (block + 1) * TOK)
        partial_ref[span, :] = out
        query_out_ref[span, :] = jnp.where(
            doc_rows == chunk_before, query * jnp.exp(cumulative + passed), 0.0
        )
        end_key = jnp.where(doc_rows == doc_last, key * jnp.exp(whole - cumulative), 0.0)
        fresh = dot(end_key, value, ((0,), (0,)), PRECISE)
        if block == 0:
            state = fresh
        else:
            kept = column(jnp.where(doc_last == doc_before, jnp.exp(whole), 0.0))
            state = jnp.concatenate([kept, kept], axis=1) * state + fresh
        passed = passed + whole
    kept = column(jnp.where(doc_last == chunk_before, jnp.exp(passed), 0.0))
    low = iota((DK, DK), 1) < DK // 2
    for part in range(4):
        piece = state[:, (part // 2) * DK : (part // 2 + 1) * DK]
        if part % 2:
            piece = pltpu.roll(piece, DK // 2, 1)
        piece = jnp.where(low, piece, kept)
        map_ref[part * 16 : (part + 1) * 16] = piece.reshape(16, 8, DK)


def scan_kernel(map_ref, prefix_ref):
    low = iota(map_ref.shape[1:], 1) < DK // 2

    def step(chunk, state):
        prefix_ref[chunk] = state
        here = map_ref[chunk]
        return jnp.where(low, pltpu.roll(here, DK // 2, 1), 0.0) * state + here

    lax.fori_loop(0, map_ref.shape[0], step, jnp.zeros(map_ref.shape[1:], F32), unroll=True)


def finish_kernel(place_ref, prefix_ref, partial_ref, query_ref, gain_ref, out_ref):
    low = iota((DK, DK), 1) < DK // 2
    parts = [prefix_ref[part * 16 : (part + 1) * 16].reshape(DK, DK) for part in range(4)]
    state = jnp.concatenate(
        [
            jnp.where(low, parts[2 * side], pltpu.roll(parts[2 * side + 1], DK // 2, 1))
            for side in range(2)
        ],
        axis=1,
    )
    gain = gain_ref[pl.ds(place_ref[3], 1), :]
    for block in range(GROUP):
        span = slice(block * TOK, (block + 1) * TOK)
        mixed = partial_ref[span, :] + dot(query_ref[span, :], state, precision=PRECISE)
        scale = lax.rsqrt(jnp.mean(mixed * mixed, axis=1, keepdims=True) + EPSILON)
        out_ref[block] = (mixed * scale * gain).astype(BF16)


SMEM = pl.BlockSpec(memory_space=pltpu.SMEM)
VMEM = pl.BlockSpec(memory_space=pltpu.VMEM)


def call(kernel, scalars, arrays, outs, cost=0):
    return pl.pallas_call(
        kernel,
        out_shape=outs,
        in_specs=[SMEM] * scalars + [VMEM] * arrays,
        out_specs=jax.tree.map(lambda _: VMEM, outs),
        compiler_params=pltpu.CompilerParams(vmem_limit_bytes=32 << 20),
        cost_estimate=pl.CostEstimate(flops=cost, bytes_accessed=1 << 20, transcendentals=0),
    )


def shape(dims, dtype=F32):
    return jax.ShapeDtypeStruct(dims, dtype)


def local(queries, key_vectors, value_vectors, decay_log, assignment, doc_lengths, norm_gain):
    own = lax.axis_index(CTX)
    place = jnp.stack([own, own // GROUP, lax.axis_index("node"), own % GROUP]).astype(jnp.int32)
    matrix = assignment[0]
    packed = call(pack_kernel, 1, 5, shape((OWNERS // GROUP, HEADS, CAP, WIDTH), BF16), 1 << 28)(
        place, matrix, queries[0], key_vectors[0], value_vectors[0], decay_log[0]
    )
    received = lax.all_to_all(packed.reshape(OWNERS, CAP, WIDTH), CTX, 0, 0, tiled=True)
    maps, partial, query = call(
        chunk_kernel,
        2,
        2,
        (shape((OWNERS, 8, DK)), shape((CHUNK, DV)), shape((CHUNK, DK))),
        1 << 30,
    )(place, doc_lengths, matrix, received)
    maps = lax.all_to_all(maps, CHUNKS, 0, 0, tiled=True)
    prefix = call(scan_kernel, 0, 1, shape((OWNERS, 8, DK)), 1 << 24)(maps)
    prefix = lax.all_to_all(prefix, CHUNKS, 0, 0, tiled=True)
    out = call(finish_kernel, 1, 4, shape((GROUP, TOK, DV), BF16), 1 << 28)(
        place, prefix, partial, query, norm_gain.reshape(HEADS, DV)
    )
    out = lax.all_to_all(out, "zl", 0, 0, tiled=True)
    return jnp.transpose(out, (1, 0, 2)).reshape(1, TOK, HEADS * DV)


def solution(mesh):
    split = Mesh(mesh.devices.reshape(4, 4, 4, 4, 2), ("y", "zh", "zl", "node", "tp"))
    rows = P("node", CTX, "tp")
    return jax.shard_map(
        local,
        mesh=split,
        in_specs=(rows, rows, rows, rows, P("node", None, None), P(), P("tp")),
        out_specs=rows,
        check_vma=False,
    )
```

```python
import jax
import jax.numpy as jnp
from jax import lax
from jax.experimental import pallas as pl
from jax.experimental.pallas import tpu as pltpu
from jax.sharding import Mesh, PartitionSpec as P

DK = 128
DV = 256
HEADS = 4
GROUP = 4
TOK = 128
CAP = 16
CHUNK = GROUP * TOK
OWNERS = 64
WIDTH = 3 * DK + DV
EPSILON = 1e-05
CTX = ("y", "zh", "zl")
REGROUP = ("zl", "zh", "y")
CHUNKS = ("node", "y", "zh")
PRECISE = lax.Precision.HIGHEST
F32 = jnp.float32
BF16 = jnp.bfloat16


def iota(shape, dim):
    return lax.broadcasted_iota(jnp.int32, shape, dim)


def dot(a, b, dims=((1,), (0,)), precision=None):
    return lax.dot_general(a, b, (dims, ((), ())), precision=precision, preferred_element_type=F32)


def pack_kernel(
    place_ref, matrix_ref, query_hbm, key_hbm, value_hbm, rate_hbm, out_ref,
    query_ref, key_ref, value_ref, rate_ref, sems,
):
    pairs = ((query_hbm, query_ref), (key_hbm, key_ref), (value_hbm, value_ref), (rate_hbm, rate_ref))
    copies = [pltpu.make_async_copy(a, b, sems.at[i]) for i, (a, b) in enumerate(pairs)]
    for copy in copies:
        copy.start()
    slots = (OWNERS // GROUP) * CAP
    counts = matrix_ref[pl.ds(place_ref[0], 1), :].astype(F32)
    nth = lax.shift_right_logical(iota((slots, OWNERS), 0), 4)
    chunk = (nth & 3) * 4 + lax.shift_right_logical(nth, 2)
    before = iota((slots, OWNERS), 1) < chunk * GROUP
    start = jnp.sum(jnp.where(before, counts, 0.0), axis=1, keepdims=True).astype(jnp.int32)
    wanted = start + (iota((slots, 1), 0) & (CAP - 1))
    pick = (iota((slots, TOK), 1) == wanted).astype(F32).astype(BF16)
    at = 0
    for copy, ref, width in zip(copies, (query_ref, key_ref, value_ref, rate_ref), (DK, DK, DV, DK)):
        copy.wait()
        rows = dot(pick, ref[...]).astype(BF16)
        for head in range(HEADS):
            piece = rows[:, head * width : (head + 1) * width]
            out_ref[head, :, :, at : at + width] = piece.reshape(slots // CAP, CAP, width)
        at += width


def doc_of(lengths_ref, places):
    end = jnp.int32(0)
    doc = jnp.zeros_like(places)
    for d in range(lengths_ref.shape[0]):
        end = end + lengths_ref[d]
        doc = doc + (end <= places).astype(jnp.int32)
    return doc


def unpack(place_ref, matrix_ref, received_ref):
    first = place_ref[1] * GROUP
    matrix = matrix_ref[...].astype(F32).astype(BF16)
    owner = iota((8, OWNERS), 1)
    nth = iota((8, OWNERS), 0)
    one = ((owner == first + nth) & (nth < GROUP)).astype(F32).astype(BF16)
    upto = ((owner >= first) & (owner <= first + nth) & (nth < GROUP)).astype(F32).astype(BF16)
    counts = dot(one, matrix, ((1,), (1,)))
    ends = dot(upto, matrix, ((1,), (1,)))
    earlier = (iota((OWNERS, OWNERS), 0) < iota((OWNERS, OWNERS), 1)).astype(F32).astype(BF16)
    arrive = dot(counts.astype(BF16), earlier)
    slots = OWNERS * CAP
    loader = iota((OWNERS, slots), 0)
    nth = (loader & 3) * 16 + (loader & 12) + lax.shift_right_logical(loader, 4)
    expand = (lax.shift_right_logical(iota((OWNERS, slots), 1), 4) == nth).astype(F32).astype(BF16)
    counts, ends, arrive = [dot(a.astype(BF16), expand) for a in (counts, ends, arrive)]
    slot = (iota((8, slots), 1) & (CAP - 1)).astype(F32)
    inside = (slot < ends) & (slot >= ends - counts)
    target = iota((8, slots), 0).astype(F32) * TOK + arrive + slot - (ends - counts) + 1.0
    target = jnp.sum(jnp.where(inside, target, 0.0), axis=0, keepdims=True).astype(jnp.int32) - 1
    pick = (iota((CHUNK, slots), 0) == target).astype(F32).astype(BF16)
    return dot(pick, received_ref[...].reshape(slots, WIDTH))


def column(row):
    return jnp.transpose(jnp.broadcast_to(row, (DK, DK)))


def decays(rate):
    tril = (iota((TOK, TOK), 0) >= iota((TOK, TOK), 1)).astype(F32)
    parts = []
    for block in range(GROUP):
        log_decay = -jnp.exp(rate[block * TOK : (block + 1) * TOK].astype(F32))
        cumulative = dot(tril, log_decay, precision=PRECISE)
        parts.append((cumulative, cumulative[TOK - 1 :, :]))
    return parts


def doc_at(lengths_ref, place):
    return doc_of(lengths_ref, jnp.full((1, 1), place, jnp.int32))


def maps_kernel(place_ref, lengths_ref, matrix_ref, received_ref, rows_ref, map_ref):
    rows_ref[...] = unpack(place_ref, matrix_ref, received_ref).astype(BF16)
    first = (place_ref[2] * (OWNERS // GROUP) + place_ref[1]) * CHUNK
    parts = decays(rows_ref[:, 2 * DK + DV :])
    after = jnp.zeros((1, DK), F32)
    end_keys = []
    for block in reversed(range(GROUP)):
        cumulative, whole = parts[block]
        key = rows_ref[block * TOK : (block + 1) * TOK, DK : 2 * DK].astype(F32)
        end_keys.insert(0, key * jnp.exp(whole - cumulative + after))
        after = after + whole
    doc_last = doc_at(lengths_ref, first + CHUNK - 1)
    doc_rows = doc_of(lengths_ref, first + iota((CHUNK, DK), 0))
    end_key = jnp.where(doc_rows == doc_last, jnp.concatenate(end_keys, axis=0), 0.0)
    value = rows_ref[:, 2 * DK : 2 * DK + DV].astype(F32)
    state = dot(end_key, value, ((0,), (0,)), PRECISE)
    kept = column(jnp.where(doc_last == doc_at(lengths_ref, first - 1), jnp.exp(after), 0.0))
    half = DK // 2
    map_ref[:, 0, :DV] = state[:half]
    map_ref[:, 0, DV : 2 * DV] = state[half:]
    map_ref[:, 0, 2 * DV :] = jnp.where(iota((half, DK), 1) < half, kept[:half], kept[half:])


def block_kernel(place_ref, lengths_ref, rows_ref, partial_ref, query_out_ref):
    first = (place_ref[2] * (OWNERS // GROUP) + place_ref[1]) * CHUNK
    state = None
    passed = jnp.zeros((1, DK), F32)
    chunk_before = doc_at(lengths_ref, first - 1)
    for block, (cumulative, whole) in enumerate(decays(rows_ref[:, 2 * DK + DV :])):
        span = slice(block * TOK, (block + 1) * TOK)
        query = rows_ref[span, :DK].astype(F32)
        key = rows_ref[span, DK : 2 * DK].astype(F32)
        value = rows_ref[span, 2 * DK : 2 * DK + DV].astype(F32)
        start = first + block * TOK
        doc_rows = doc_of(lengths_ref, start + iota((TOK, DK), 0))
        doc_columns = doc_of(lengths_ref, start + iota((TOK, TOK), 1))
        doc_before = doc_at(lengths_ref, start - 1)
        doc_last = doc_at(lengths_ref, start + TOK - 1)
        half = 0.5 * whole
        scores = dot(
            query * jnp.exp(cumulative - half),
            key * jnp.exp(half - cumulative),
            ((1,), (1,)),
            PRECISE,
        )
        allowed = (iota((TOK, TOK), 0) >= iota((TOK, TOK), 1)) & (doc_rows == doc_columns)
        out = dot(jnp.where(allowed, scores, 0.0), value, precision=PRECISE)
        if block > 0:
            kept = jnp.where(doc_rows == doc_before, query * jnp.exp(cumulative), 0.0)
            out = out + dot(kept, state, precision=PRECISE)
        partial_ref[span, :] = out
        query_out_ref[span, :] = jnp.where(
            doc_rows == chunk_before, query * jnp.exp(cumulative + passed), 0.0
        )
        if block < GROUP - 1:
            end_key = jnp.where(doc_rows == doc_last, key * jnp.exp(whole - cumulative), 0.0)
            fresh = dot(end_key, value, ((0,), (0,)), PRECISE)
            if block == 0:
                state = fresh
            else:
                kept = column(jnp.where(doc_last == doc_before, jnp.exp(whole), 0.0))
                state = jnp.concatenate([kept, kept], axis=1) * state + fresh
        passed = passed + whole


def scan_kernel(map_ref, prefix_ref):
    low = iota((1, DK), 1) < DK // 2

    def step(chunk, state):
        prefix_ref[chunk] = state
        here = map_ref[chunk]
        kept = here[:, 2 * DV :]
        other = pltpu.roll(kept, DK // 2, 1)
        one, two = jnp.where(low, kept, other), jnp.where(low, other, kept)
        return jnp.concatenate([one, one, two, two], axis=1) * state + here[:, : 2 * DV]

    lax.fori_loop(0, map_ref.shape[0], step, jnp.zeros((1, 2 * DV), F32), unroll=True)


def finish_kernel(place_ref, prefix_ref, partial_ref, query_ref, gain_ref, out_ref):
    state = jnp.concatenate([prefix_ref[:, 0, :DV], prefix_ref[:, 0, DV:]], axis=0)
    gain = gain_ref[pl.ds(place_ref[3], 1), :]
    for block in range(GROUP):
        span = slice(block * TOK, (block + 1) * TOK)
        mixed = partial_ref[span, :] + dot(query_ref[span, :], state, precision=PRECISE)
        scale = lax.rsqrt(jnp.mean(mixed * mixed, axis=1, keepdims=True) + EPSILON)
        out_ref[block] = (mixed * scale * gain).astype(BF16)


SMEM = pl.BlockSpec(memory_space=pltpu.SMEM)
VMEM = pl.BlockSpec(memory_space=pltpu.VMEM)
HBM = pl.BlockSpec(memory_space=pltpu.HBM)


def call(kernel, specs, outs, cost=0, scratch=()):
    return pl.pallas_call(
        kernel,
        out_shape=outs,
        in_specs=specs,
        out_specs=jax.tree.map(lambda _: VMEM, outs),
        scratch_shapes=scratch,
        compiler_params=pltpu.CompilerParams(vmem_limit_bytes=32 << 20),
        cost_estimate=pl.CostEstimate(flops=cost, bytes_accessed=1 << 20, transcendentals=0),
    )


def shape(dims, dtype=F32):
    return jax.ShapeDtypeStruct(dims, dtype)


def local(queries, key_vectors, value_vectors, decay_log, assignment, doc_lengths, norm_gain):
    own = lax.axis_index(CTX)
    place = jnp.stack([own, own // GROUP, lax.axis_index("node"), own % GROUP]).astype(jnp.int32)
    matrix = assignment[0]
    streams = (queries[0], key_vectors[0], value_vectors[0], decay_log[0])
    packed = call(
        pack_kernel,
        [SMEM, VMEM] + [HBM] * 4,
        shape((HEADS, OWNERS // GROUP, CAP, WIDTH), BF16),
        1 << 28,
        [pltpu.VMEM(a.shape, BF16) for a in streams] + [pltpu.SemaphoreType.DMA((4,))],
    )(place, matrix, *streams)
    received = lax.all_to_all(packed.reshape(OWNERS, CAP, WIDTH), REGROUP, 0, 0, tiled=True)
    rows, maps = call(
        maps_kernel,
        [SMEM, SMEM, VMEM, VMEM],
        (shape((CHUNK, WIDTH), BF16), shape((OWNERS, 1, 2 * DV + DK))),
        1 << 29,
    )(place, doc_lengths, matrix, received)
    maps = lax.all_to_all(maps, CHUNKS, 0, 0, tiled=True)
    partial, query = call(
        block_kernel,
        [SMEM, SMEM, VMEM],
        (shape((CHUNK, DV)), shape((CHUNK, DK))),
        1 << 30,
    )(place, doc_lengths, rows)
    prefix = call(scan_kernel, [VMEM], shape((OWNERS, 1, 2 * DV)), 1 << 24)(maps)
    prefix = lax.all_to_all(prefix, CHUNKS, 0, 0, tiled=True)
    out = call(finish_kernel, [SMEM] + [VMEM] * 4, shape((GROUP, TOK, DV), BF16), 1 << 28)(
        place, prefix, partial, query, norm_gain.reshape(HEADS, DV)
    )
    out = lax.all_to_all(out, "zl", 0, 0, tiled=True)
    return jnp.transpose(out, (1, 0, 2)).reshape(1, TOK, HEADS * DV)


def solution(mesh):
    split = Mesh(mesh.devices.reshape(4, 4, 4, 4, 2), ("y", "zh", "zl", "node", "tp"))
    rows = P("node", CTX, "tp")
    return jax.shard_map(
        local,
        mesh=split,
        in_specs=(rows, rows, rows, rows, P("node", None, None), P(), P("tp")),
        out_specs=rows,
        check_vma=False,
    )
```

```python
import jax
import jax.numpy as jnp
from jax import lax
from jax.experimental import pallas as pl
from jax.experimental.pallas import tpu as pltpu
from jax.sharding import Mesh, PartitionSpec as P

DK = 128
DV = 256
HEADS = 4
GROUP = 4
TOK = 128
CAP = 16
CHUNK = GROUP * TOK
OWNERS = 64
LATE = 2 * DK + DV
WIDTH = LATE + DK
EPSILON = 1e-05
CTX = ("y", "zh", "zl")
REGROUP = ("zl", "zh", "y")
CHUNKS = ("node", "y", "zh")
PRECISE = lax.Precision.HIGHEST
F32 = jnp.float32
BF16 = jnp.bfloat16


def iota(shape, dim):
    return lax.broadcasted_iota(jnp.int32, shape, dim)


def dot(a, b, dims=((1,), (0,)), precision=None):
    return lax.dot_general(a, b, (dims, ((), ())), precision=precision, preferred_element_type=F32)


def split(a):
    high = a.astype(BF16)
    rest = a - high.astype(F32)
    middle = rest.astype(BF16)
    return high, middle, (rest - middle.astype(F32)).astype(BF16)


def dot_left(a, b, dims=((1,), (0,))):
    high, middle, low = split(a)
    return dot(high, b, dims) + (dot(middle, b, dims) + dot(low, b, dims))


def pack_kernel(
    matrix_hbm, query_hbm, key_hbm, value_hbm, rate_hbm, out_ref,
    matrix_ref, query_ref, key_ref, value_ref, rate_ref, sems,
):
    sources = (matrix_hbm, key_hbm, rate_hbm, value_hbm, query_hbm)
    targets = (matrix_ref, key_ref, rate_ref, value_ref, query_ref)
    copies = [pltpu.make_async_copy(a, b, sems.at[i]) for i, (a, b) in enumerate(zip(sources, targets))]
    for copy in copies:
        copy.start()
    copies[0].wait()
    slots = (OWNERS // GROUP) * CAP
    counts = matrix_ref[pl.ds(lax.axis_index(CTX), 1), :].astype(F32)
    nth = lax.shift_right_logical(iota((slots, OWNERS), 0), 4)
    chunk = (nth & 3) * 4 + lax.shift_right_logical(nth, 2)
    before = iota((slots, OWNERS), 1) < chunk * GROUP
    start = jnp.sum(jnp.where(before, counts, 0.0), axis=1, keepdims=True).astype(jnp.int32)
    wanted = start + (iota((slots, 1), 0) & (CAP - 1))
    pick = (iota((slots, TOK), 1) == wanted).astype(F32).astype(BF16)
    at = 0
    for copy, ref, width in zip(copies[1:], targets[1:], (DK, DK, DV, DK)):
        copy.wait()
        rows = dot(pick, ref[...]).astype(BF16)
        for head in range(HEADS):
            piece = rows[:, head * width : (head + 1) * width]
            out_ref[head, :, :, at : at + width] = piece.reshape(slots // CAP, CAP, width)
        at += width


def chunk_in_group():
    return lax.axis_index("y") * 4 + lax.axis_index("zh")


def chunk_start():
    return (lax.axis_index("node") * (OWNERS // GROUP) + chunk_in_group()) * CHUNK


def doc_of(lengths_ref, places):
    end = jnp.int32(0)
    doc = jnp.zeros_like(places)
    for d in range(lengths_ref.shape[0]):
        end = end + lengths_ref[d]
        doc = doc + (end <= places).astype(jnp.int32)
    return doc


def slot_targets(matrix_ref):
    first = chunk_in_group() * GROUP
    matrix = matrix_ref[...].astype(F32).astype(BF16)
    owner = iota((8, OWNERS), 1)
    nth = iota((8, OWNERS), 0)
    one = ((owner == first + nth) & (nth < GROUP)).astype(F32).astype(BF16)
    upto = ((owner >= first) & (owner <= first + nth) & (nth < GROUP)).astype(F32).astype(BF16)
    counts = dot(one, matrix, ((1,), (1,)))
    ends = dot(upto, matrix, ((1,), (1,)))
    earlier = (iota((OWNERS, OWNERS), 0) < iota((OWNERS, OWNERS), 1)).astype(F32).astype(BF16)
    arrive = dot(counts.astype(BF16), earlier)
    slots = OWNERS * CAP
    loader = iota((OWNERS, slots), 0)
    nth = (loader & 3) * 16 + (loader & 12) + lax.shift_right_logical(loader, 4)
    expand = (lax.shift_right_logical(iota((OWNERS, slots), 1), 4) == nth).astype(F32).astype(BF16)
    wide = dot(jnp.concatenate([counts, ends, arrive], axis=0).astype(BF16), expand)
    counts, ends, arrive = wide[:8], wide[8:16], wide[16:]
    slot = (iota((8, slots), 1) & (CAP - 1)).astype(F32)
    inside = (slot < ends) & (slot >= ends - counts)
    target = iota((8, slots), 0).astype(F32) * TOK + arrive + slot - (ends - counts) + 1.0
    return jnp.sum(jnp.where(inside, target, 0.0), axis=0, keepdims=True).astype(jnp.int32) - 1


def unpack(targets, received):
    pick = (iota((CHUNK, OWNERS * CAP), 0) == targets).astype(F32).astype(BF16)
    return dot(pick, received.reshape(OWNERS * CAP, received.shape[2])).astype(BF16)


def column(row):
    return jnp.transpose(jnp.broadcast_to(row, (DK, DK)))


def decays(rate):
    rate = jnp.concatenate([rate[i * TOK : (i + 1) * TOK] for i in range(GROUP)], axis=1)
    tril = (iota((TOK, TOK), 0) >= iota((TOK, TOK), 1)).astype(F32).astype(BF16)
    high, middle, low = split(-jnp.exp(rate.astype(F32)))
    cumulative = dot(tril, high) + (dot(tril, middle) + dot(tril, low))
    parts = [cumulative[:, i * DK : (i + 1) * DK] for i in range(GROUP)]
    return [(part, part[TOK - 1 :, :]) for part in parts]


def doc_at(lengths_ref, place):
    return doc_of(lengths_ref, jnp.full((1, 1), place, jnp.int32))


def maps_kernel(lengths_ref, matrix_ref, received_ref, rows_ref, targets_ref, map_ref):
    targets = slot_targets(matrix_ref)
    targets_ref[...] = targets
    rows_ref[...] = unpack(targets, received_ref[:, :, :LATE])
    first = chunk_start()
    parts = decays(rows_ref[:, DK : 2 * DK])
    after = jnp.zeros((1, DK), F32)
    end_keys = []
    for block in reversed(range(GROUP)):
        cumulative, whole = parts[block]
        key = rows_ref[block * TOK : (block + 1) * TOK, :DK].astype(F32)
        end_keys.insert(0, key * jnp.exp(whole - cumulative + after))
        after = after + whole
    doc_last = doc_at(lengths_ref, first + CHUNK - 1)
    doc_rows = doc_of(lengths_ref, first + iota((CHUNK, DK), 0))
    end_key = jnp.where(doc_rows == doc_last, jnp.concatenate(end_keys, axis=0), 0.0)
    state = dot_left(end_key, rows_ref[:, 2 * DK :], ((0,), (0,)))
    kept = column(jnp.where(doc_last == doc_at(lengths_ref, first - 1), jnp.exp(after), 0.0))
    half = DK // 2
    map_ref[:, 0, :DV] = state[:half]
    map_ref[:, 0, DV : 2 * DV] = state[half:]
    map_ref[:, 0, 2 * DV :] = jnp.where(iota((half, DK), 1) < half, kept[:half], kept[half:])


def block_kernel(lengths_ref, targets_ref, received_ref, rows_ref, partial_ref, query_out_ref):
    first = chunk_start()
    queries = unpack(targets_ref[...], received_ref[:, :, LATE:])
    state = None
    passed = jnp.zeros((1, DK), F32)
    chunk_before = doc_at(lengths_ref, first - 1)
    for block, (cumulative, whole) in enumerate(decays(rows_ref[:, DK : 2 * DK])):
        span = slice(block * TOK, (block + 1) * TOK)
        query = queries[span].astype(F32)
        key = rows_ref[span, :DK].astype(F32)
        value = rows_ref[span, 2 * DK :]
        start = first + block * TOK
        doc_rows = doc_of(lengths_ref, start + iota((TOK, DK), 0))
        doc_columns = doc_of(lengths_ref, start + iota((TOK, TOK), 1))
        doc_before = doc_at(lengths_ref, start - 1)
        doc_last = doc_at(lengths_ref, start + TOK - 1)
        half = 0.5 * whole
        scores = dot(
            query * jnp.exp(cumulative - half),
            key * jnp.exp(half - cumulative),
            ((1,), (1,)),
            PRECISE,
        )
        allowed = (iota((TOK, TOK), 0) >= iota((TOK, TOK), 1)) & (doc_rows == doc_columns)
        out = dot_left(jnp.where(allowed, scores, 0.0), value)
        if block > 0:
            kept = jnp.where(doc_rows == doc_before, query * jnp.exp(cumulative), 0.0)
            out = out + dot(kept, state, precision=PRECISE)
        partial_ref[span, :] = out
        query_out_ref[span, :] = jnp.where(
            doc_rows == chunk_before, query * jnp.exp(cumulative + passed), 0.0
        )
        if block < GROUP - 1:
            end_key = jnp.where(doc_rows == doc_last, key * jnp.exp(whole - cumulative), 0.0)
            fresh = dot_left(end_key, value, ((0,), (0,)))
            if block == 0:
                state = fresh
            else:
                kept = column(jnp.where(doc_last == doc_before, jnp.exp(whole), 0.0))
                state = jnp.concatenate([kept, kept], axis=1) * state + fresh
        passed = passed + whole


def scan_kernel(map_ref, prefix_ref):
    low = iota((1, DK), 1) < DK // 2

    def step(chunk, state):
        prefix_ref[chunk] = state
        here = map_ref[chunk]
        kept = here[:, 2 * DV :]
        other = pltpu.roll(kept, DK // 2, 1)
        one, two = jnp.where(low, kept, other), jnp.where(low, other, kept)
        return jnp.concatenate([one, one, two, two], axis=1) * state + here[:, : 2 * DV]

    lax.fori_loop(0, map_ref.shape[0], step, jnp.zeros((1, 2 * DV), F32), unroll=True)


def finish_kernel(prefix_ref, partial_ref, query_ref, gain_ref, out_ref):
    state = jnp.concatenate([prefix_ref[:, 0, :DV], prefix_ref[:, 0, DV:]], axis=0)
    gain = gain_ref[pl.ds(lax.axis_index("zl"), 1), :]
    for block in range(GROUP):
        span = slice(block * TOK, (block + 1) * TOK)
        mixed = partial_ref[span, :] + dot(query_ref[span, :], state, precision=PRECISE)
        scale = lax.rsqrt(jnp.mean(mixed * mixed, axis=1, keepdims=True) + EPSILON)
        out_ref[block] = (mixed * scale * gain).astype(BF16)


SMEM = pl.BlockSpec(memory_space=pltpu.SMEM)
VMEM = pl.BlockSpec(memory_space=pltpu.VMEM)
HBM = pl.BlockSpec(memory_space=pltpu.HBM)


def call(kernel, specs, outs, cost=0, scratch=(), limit=32 << 20):
    return pl.pallas_call(
        kernel,
        out_shape=outs,
        in_specs=specs,
        out_specs=jax.tree.map(lambda _: VMEM, outs),
        scratch_shapes=scratch,
        compiler_params=pltpu.CompilerParams(vmem_limit_bytes=limit),
        cost_estimate=pl.CostEstimate(flops=cost, bytes_accessed=1 << 20, transcendentals=0),
    )


def shape(dims, dtype=F32):
    return jax.ShapeDtypeStruct(dims, dtype)


def local(queries, key_vectors, value_vectors, decay_log, assignment, doc_lengths, norm_gain):
    matrix = assignment[0]
    streams = (matrix, queries[0], key_vectors[0], value_vectors[0], decay_log[0])
    packed = call(
        pack_kernel,
        [HBM] * 5,
        shape((HEADS, OWNERS // GROUP, CAP, WIDTH), BF16),
        1 << 28,
        [pltpu.VMEM(a.shape, a.dtype) for a in streams] + [pltpu.SemaphoreType.DMA((5,))],
        65500000,
    )(*streams)
    received = lax.all_to_all(packed.reshape(OWNERS, CAP, WIDTH), REGROUP, 0, 0, tiled=True)
    rows, targets, maps = call(
        maps_kernel,
        [SMEM, VMEM, VMEM],
        (
            shape((CHUNK, LATE), BF16),
            shape((1, OWNERS * CAP), jnp.int32),
            shape((OWNERS, 1, 2 * DV + DK)),
        ),
        1 << 29,
    )(doc_lengths, matrix, received)
    maps = lax.all_to_all(maps, CHUNKS, 0, 0, tiled=True)
    partial, query = call(
        block_kernel,
        [SMEM, VMEM, VMEM, VMEM],
        (shape((CHUNK, DV)), shape((CHUNK, DK))),
        1 << 30,
    )(doc_lengths, targets, received, rows)
    prefix = call(scan_kernel, [VMEM], shape((OWNERS, 1, 2 * DV)), 1 << 24)(maps)
    prefix = lax.all_to_all(prefix, CHUNKS, 0, 0, tiled=True)
    out = call(finish_kernel, [VMEM] * 4, shape((GROUP, TOK, DV), BF16), 1 << 28)(
        prefix, partial, query, norm_gain.reshape(HEADS, DV)
    )
    out = lax.all_to_all(out, "zl", 0, 0, tiled=True)
    return jnp.transpose(out, (1, 0, 2)).reshape(1, TOK, HEADS * DV)


def solution(mesh):
    split = Mesh(mesh.devices.reshape(4, 4, 4, 4, 2), ("y", "zh", "zl", "node", "tp"))
    rows = P("node", CTX, "tp")
    return jax.shard_map(
        local,
        mesh=split,
        in_specs=(rows, rows, rows, rows, P("node", None, None), P(), P("tp")),
        out_specs=rows,
        check_vma=False,
    )
```

```python
import jax
import jax.numpy as jnp
from jax import lax
from jax.experimental import pallas as pl
from jax.experimental.pallas import tpu as pltpu
from jax.sharding import Mesh, PartitionSpec as P

DK = 128
DV = 256
HEADS = 4
GROUP = 4
TOK = 128
CAP = 16
CHUNK = GROUP * TOK
OWNERS = 64
LATE = 2 * DK + DV
WIDTH = LATE + DK
EPSILON = 1e-05
CTX = ("y", "zh", "zl")
REGROUP = ("zl", "zh", "y")
CHUNKS = ("zh", "node", "y")
PRECISE = lax.Precision.HIGHEST
F32 = jnp.float32
BF16 = jnp.bfloat16


def iota(shape, dim):
    return lax.broadcasted_iota(jnp.int32, shape, dim)


def dot(a, b, dims=((1,), (0,)), precision=None):
    return lax.dot_general(a, b, (dims, ((), ())), precision=precision, preferred_element_type=F32)


def split(a):
    high = a.astype(BF16)
    rest = a - high.astype(F32)
    middle = rest.astype(BF16)
    return high, middle, (rest - middle.astype(F32)).astype(BF16)


def dot_left(a, b, dims=((1,), (0,))):
    high, middle, low = split(a)
    return dot(high, b, dims) + (dot(middle, b, dims) + dot(low, b, dims))


def pack_kernel(
    matrix_hbm, query_hbm, key_hbm, value_hbm, rate_hbm, out_ref,
    matrix_ref, query_ref, key_ref, value_ref, rate_ref, sems,
):
    sources = (matrix_hbm, key_hbm, rate_hbm, value_hbm, query_hbm)
    targets = (matrix_ref, key_ref, rate_ref, value_ref, query_ref)
    copies = [pltpu.make_async_copy(a, b, sems.at[i]) for i, (a, b) in enumerate(zip(sources, targets))]
    for copy in copies:
        copy.start()
    copies[0].wait()
    slots = (OWNERS // GROUP) * CAP
    counts = matrix_ref[pl.ds(lax.axis_index(CTX), 1), :].astype(F32)
    nth = lax.shift_right_logical(iota((slots, OWNERS), 0), 4)
    chunk = (nth & 3) * 4 + lax.shift_right_logical(nth, 2)
    before = iota((slots, OWNERS), 1) < chunk * GROUP
    start = jnp.sum(jnp.where(before, counts, 0.0), axis=1, keepdims=True).astype(jnp.int32)
    wanted = start + (iota((slots, 1), 0) & (CAP - 1))
    pick = (iota((slots, TOK), 1) == wanted).astype(F32).astype(BF16)
    at = 0
    for copy, ref, width in zip(copies[1:], targets[1:], (DK, DK, DV, DK)):
        copy.wait()
        rows = dot(pick, ref[...]).astype(BF16)
        for head in range(HEADS):
            piece = rows[:, head * width : (head + 1) * width]
            out_ref[head, :, :, at : at + width] = piece.reshape(slots // CAP, CAP, width)
        at += width


def chunk_in_group():
    return lax.axis_index("y") * 4 + lax.axis_index("zh")


def chunk_start():
    return (lax.axis_index("node") * (OWNERS // GROUP) + chunk_in_group()) * CHUNK


def doc_of(lengths_ref, places):
    end = jnp.int32(0)
    doc = jnp.zeros_like(places)
    for d in range(lengths_ref.shape[0]):
        end = end + lengths_ref[d]
        doc = doc + (end <= places).astype(jnp.int32)
    return doc


def slot_targets(matrix_ref):
    first = chunk_in_group() * GROUP
    matrix = matrix_ref[...].astype(F32).astype(BF16)
    owner = iota((8, OWNERS), 1)
    nth = iota((8, OWNERS), 0)
    one = ((owner == first + nth) & (nth < GROUP)).astype(F32).astype(BF16)
    upto = ((owner >= first) & (owner <= first + nth) & (nth < GROUP)).astype(F32).astype(BF16)
    counts = dot(one, matrix, ((1,), (1,)))
    ends = dot(upto, matrix, ((1,), (1,)))
    earlier = (iota((OWNERS, OWNERS), 0) < iota((OWNERS, OWNERS), 1)).astype(F32).astype(BF16)
    arrive = dot(counts.astype(BF16), earlier)
    slots = OWNERS * CAP
    loader = iota((OWNERS, slots), 0)
    nth = (loader & 3) * 16 + (loader & 12) + lax.shift_right_logical(loader, 4)
    expand = (lax.shift_right_logical(iota((OWNERS, slots), 1), 4) == nth).astype(F32).astype(BF16)
    wide = dot(jnp.concatenate([counts, ends, arrive], axis=0).astype(BF16), expand)
    counts, ends, arrive = wide[:8], wide[8:16], wide[16:]
    slot = (iota((8, slots), 1) & (CAP - 1)).astype(F32)
    inside = (slot < ends) & (slot >= ends - counts)
    target = iota((8, slots), 0).astype(F32) * TOK + arrive + slot - (ends - counts) + 1.0
    return jnp.sum(jnp.where(inside, target, 0.0), axis=0, keepdims=True).astype(jnp.int32) - 1


def place_kernel(matrix_ref, pick_ref):
    targets = slot_targets(matrix_ref)
    pick_ref[...] = (iota((CHUNK, OWNERS * CAP), 0) == targets).astype(F32).astype(BF16)


def unpack(pick, received):
    return dot(pick, received.reshape(OWNERS * CAP, received.shape[2])).astype(BF16)


def column(row):
    return jnp.transpose(jnp.broadcast_to(row, (DK, DK)))


def decays(rate):
    rate = jnp.concatenate([rate[i * TOK : (i + 1) * TOK] for i in range(GROUP)], axis=1)
    tril = (iota((TOK, TOK), 0) >= iota((TOK, TOK), 1)).astype(F32).astype(BF16)
    high, middle, low = split(-jnp.exp(rate.astype(F32)))
    cumulative = dot(tril, high) + (dot(tril, middle) + dot(tril, low))
    parts = [cumulative[:, i * DK : (i + 1) * DK] for i in range(GROUP)]
    return [(part, part[TOK - 1 :, :]) for part in parts]


def doc_at(lengths_ref, place):
    return doc_of(lengths_ref, jnp.full((1, 1), place, jnp.int32))


def maps_kernel(lengths_ref, pick_ref, received_ref, rows_ref, map_ref):
    rows_ref[...] = unpack(pick_ref[...], received_ref[:, :, :LATE])
    first = chunk_start()
    parts = decays(rows_ref[:, DK : 2 * DK])
    after = jnp.zeros((1, DK), F32)
    end_keys = []
    for block in reversed(range(GROUP)):
        cumulative, whole = parts[block]
        key = rows_ref[block * TOK : (block + 1) * TOK, :DK].astype(F32)
        end_keys.insert(0, key * jnp.exp(whole - cumulative + after))
        after = after + whole
    doc_last = doc_at(lengths_ref, first + CHUNK - 1)
    doc_rows = doc_of(lengths_ref, first + iota((CHUNK, DK), 0))
    end_key = jnp.where(doc_rows == doc_last, jnp.concatenate(end_keys, axis=0), 0.0)
    state = dot_left(end_key, rows_ref[:, 2 * DK :], ((0,), (0,)))
    kept = column(jnp.where(doc_last == doc_at(lengths_ref, first - 1), jnp.exp(after), 0.0))
    half = DK // 2
    map_ref[:, 0, :DV] = state[:half]
    map_ref[:, 0, DV : 2 * DV] = state[half:]
    map_ref[:, 0, 2 * DV :] = jnp.where(iota((half, DK), 1) < half, kept[:half], kept[half:])


def block_kernel(lengths_ref, pick_ref, received_ref, rows_ref, partial_ref, query_out_ref):
    first = chunk_start()
    queries = unpack(pick_ref[...], received_ref[:, :, LATE:])
    state = None
    passed = jnp.zeros((1, DK), F32)
    chunk_before = doc_at(lengths_ref, first - 1)
    for block, (cumulative, whole) in enumerate(decays(rows_ref[:, DK : 2 * DK])):
        span = slice(block * TOK, (block + 1) * TOK)
        query = queries[span].astype(F32)
        key = rows_ref[span, :DK].astype(F32)
        value = rows_ref[span, 2 * DK :]
        start = first + block * TOK
        doc_rows = doc_of(lengths_ref, start + iota((TOK, DK), 0))
        doc_columns = doc_of(lengths_ref, start + iota((TOK, TOK), 1))
        doc_before = doc_at(lengths_ref, start - 1)
        doc_last = doc_at(lengths_ref, start + TOK - 1)
        half = 0.5 * whole
        scores = dot(
            query * jnp.exp(cumulative - half),
            key * jnp.exp(half - cumulative),
            ((1,), (1,)),
            PRECISE,
        )
        allowed = (iota((TOK, TOK), 0) >= iota((TOK, TOK), 1)) & (doc_rows == doc_columns)
        out = dot_left(jnp.where(allowed, scores, 0.0), value)
        if block > 0:
            kept = jnp.where(doc_rows == doc_before, query * jnp.exp(cumulative), 0.0)
            out = out + dot(kept, state, precision=PRECISE)
        partial_ref[span, :] = out
        query_out_ref[span, :] = jnp.where(
            doc_rows == chunk_before, query * jnp.exp(cumulative + passed), 0.0
        )
        if block < GROUP - 1:
            end_key = jnp.where(doc_rows == doc_last, key * jnp.exp(whole - cumulative), 0.0)
            fresh = dot_left(end_key, value, ((0,), (0,)))
            if block == 0:
                state = fresh
            else:
                kept = column(jnp.where(doc_last == doc_before, jnp.exp(whole), 0.0))
                state = jnp.concatenate([kept, kept], axis=1) * state + fresh
        passed = passed + whole


def scan_kernel(map_ref, prefix_ref):
    rows = map_ref.shape[0] // GROUP
    low = iota((rows, DK), 1) < DK // 2
    state = jnp.zeros((rows, 2 * DV), F32)
    kept = jnp.ones((rows, 2 * DV), F32)
    inside = []
    for nth in range(GROUP):
        inside.append((kept, state))
        here = map_ref[nth * rows : (nth + 1) * rows, 0, :]
        own = here[:, 2 * DV :]
        other = pltpu.roll(own, DK // 2, 1)
        one, two = jnp.where(low, own, other), jnp.where(low, other, own)
        own = jnp.concatenate([one, one, two, two], axis=1)
        state = own * state + here[:, : 2 * DV]
        kept = own * kept
    row = iota((rows, 2 * DV), 0)
    step = 1
    while step < rows:
        state = kept * jnp.where(row < step, 0.0, pltpu.roll(state, step, 0)) + state
        kept = kept * jnp.where(row < step, 1.0, pltpu.roll(kept, step, 0))
        step *= 2
    before = jnp.where(row < 1, 0.0, pltpu.roll(state, 1, 0))
    for nth, (kept, state) in enumerate(inside):
        prefix_ref[nth * rows : (nth + 1) * rows, 0, :] = kept * before + state


def finish_kernel(prefix_ref, partial_ref, query_ref, gain_ref, out_ref):
    state = jnp.concatenate([prefix_ref[:, 0, :DV], prefix_ref[:, 0, DV:]], axis=0)
    gain = gain_ref[pl.ds(lax.axis_index("zl"), 1), :]
    for block in range(GROUP):
        span = slice(block * TOK, (block + 1) * TOK)
        mixed = partial_ref[span, :] + dot(query_ref[span, :], state, precision=PRECISE)
        scale = lax.rsqrt(jnp.mean(mixed * mixed, axis=1, keepdims=True) + EPSILON)
        out_ref[block] = (mixed * scale * gain).astype(BF16)


SMEM = pl.BlockSpec(memory_space=pltpu.SMEM)
VMEM = pl.BlockSpec(memory_space=pltpu.VMEM)
HBM = pl.BlockSpec(memory_space=pltpu.HBM)


def call(kernel, specs, outs, cost=0, scratch=(), limit=32 << 20):
    return pl.pallas_call(
        kernel,
        out_shape=outs,
        in_specs=specs,
        out_specs=jax.tree.map(lambda _: VMEM, outs),
        scratch_shapes=scratch,
        compiler_params=pltpu.CompilerParams(vmem_limit_bytes=limit),
        cost_estimate=pl.CostEstimate(flops=cost, bytes_accessed=1 << 20, transcendentals=0),
    )


def shape(dims, dtype=F32):
    return jax.ShapeDtypeStruct(dims, dtype)


def local(queries, key_vectors, value_vectors, decay_log, assignment, doc_lengths, norm_gain):
    matrix = assignment[0]
    streams = (matrix, queries[0], key_vectors[0], value_vectors[0], decay_log[0])
    packed = call(
        pack_kernel,
        [HBM] * 5,
        shape((HEADS, OWNERS // GROUP, CAP, WIDTH), BF16),
        1 << 28,
        [pltpu.VMEM(a.shape, a.dtype) for a in streams] + [pltpu.SemaphoreType.DMA((5,))],
        65500000,
    )(*streams)
    received = lax.all_to_all(packed.reshape(OWNERS, CAP, WIDTH), REGROUP, 0, 0, tiled=True)
    pick = call(place_kernel, [VMEM], shape((CHUNK, OWNERS * CAP), BF16), 1 << 28)(matrix)
    rows, maps = call(
        maps_kernel,
        [SMEM, VMEM, VMEM],
        (shape((CHUNK, LATE), BF16), shape((OWNERS, 1, 2 * DV + DK))),
        1 << 29,
    )(doc_lengths, pick, received)
    maps = lax.all_to_all(maps, CHUNKS, 0, 0, tiled=True)
    partial, query = call(
        block_kernel,
        [SMEM, VMEM, VMEM, VMEM],
        (shape((CHUNK, DV)), shape((CHUNK, DK))),
        1 << 30,
    )(doc_lengths, pick, received, rows)
    prefix = call(scan_kernel, [VMEM], shape((OWNERS, 1, 2 * DV)), 1 << 24)(maps)
    prefix = lax.all_to_all(prefix, CHUNKS, 0, 0, tiled=True)
    out = call(finish_kernel, [VMEM] * 4, shape((GROUP, TOK, DV), BF16), 1 << 28)(
        prefix, partial, query, norm_gain.reshape(HEADS, DV)
    )
    out = lax.all_to_all(out, "zl", 0, 0, tiled=True)
    return jnp.transpose(out, (1, 0, 2)).reshape(1, TOK, HEADS * DV)


def solution(mesh):
    split = Mesh(mesh.devices.reshape(4, 4, 4, 4, 2), ("y", "zh", "zl", "node", "tp"))
    rows = P("node", CTX, "tp")
    return jax.shard_map(
        local,
        mesh=split,
        in_specs=(rows, rows, rows, rows, P("node", None, None), P(), P("tp")),
        out_specs=rows,
        check_vma=False,
    )
```

```python
import jax
import jax.numpy as jnp
from jax import lax
from jax.experimental import pallas as pl
from jax.experimental.pallas import tpu as pltpu
from jax.sharding import Mesh, PartitionSpec as P

DK = 128
DV = 256
HEADS = 4
GROUP = 4
TOK = 128
CAP = 16
CHUNK = GROUP * TOK
OWNERS = 64
LATE = 2 * DK + DV
WIDTH = LATE + DK
EPSILON = 1e-05
CTX = ("y", "zh", "zl")
REGROUP = ("zl", "zh", "y")
CHUNKS = ("zl", "node", "y")
PRECISE = lax.Precision.HIGHEST
F32 = jnp.float32
BF16 = jnp.bfloat16


def iota(shape, dim):
    return lax.broadcasted_iota(jnp.int32, shape, dim)


def dot(a, b, dims=((1,), (0,)), precision=None):
    return lax.dot_general(a, b, (dims, ((), ())), precision=precision, preferred_element_type=F32)


def split(a):
    high = a.astype(BF16)
    rest = a - high.astype(F32)
    middle = rest.astype(BF16)
    return high, middle, (rest - middle.astype(F32)).astype(BF16)


def dot_left(a, b, dims=((1,), (0,))):
    high, middle, low = split(a)
    return dot(high, b, dims) + (dot(middle, b, dims) + dot(low, b, dims))


def pack_kernel(
    matrix_hbm, query_hbm, key_hbm, value_hbm, rate_hbm, out_ref,
    matrix_ref, query_ref, key_ref, value_ref, rate_ref, sems,
):
    sources = (matrix_hbm, key_hbm, rate_hbm, value_hbm, query_hbm)
    targets = (matrix_ref, key_ref, rate_ref, value_ref, query_ref)
    copies = [pltpu.make_async_copy(a, b, sems.at[i]) for i, (a, b) in enumerate(zip(sources, targets))]
    for copy in copies:
        copy.start()
    copies[0].wait()
    slots = (OWNERS // GROUP) * CAP
    counts = matrix_ref[pl.ds(lax.axis_index(CTX), 1), :].astype(F32)
    nth = lax.shift_right_logical(iota((slots, OWNERS), 0), 4)
    chunk = (nth & 3) * 4 + lax.shift_right_logical(nth, 2)
    before = iota((slots, OWNERS), 1) < chunk * GROUP
    start = jnp.sum(jnp.where(before, counts, 0.0), axis=1, keepdims=True).astype(jnp.int32)
    wanted = start + (iota((slots, 1), 0) & (CAP - 1))
    pick = (iota((slots, TOK), 1) == wanted).astype(F32).astype(BF16)
    at = 0
    for copy, ref, width in zip(copies[1:], targets[1:], (DK, DK, DV, DK)):
        copy.wait()
        rows = dot(pick, ref[...]).astype(BF16)
        for head in range(HEADS):
            piece = rows[:, head * width : (head + 1) * width]
            out_ref[:, head, :, :, at : at + width] = piece.reshape(4, 4, CAP, width)
        at += width


def chunk_in_group():
    return lax.axis_index("y") * 4 + lax.axis_index("zl")


def chunk_start():
    return (lax.axis_index("node") * (OWNERS // GROUP) + chunk_in_group()) * CHUNK


def doc_of(lengths_ref, places):
    end = jnp.int32(0)
    doc = jnp.zeros_like(places)
    for d in range(lengths_ref.shape[0]):
        end = end + lengths_ref[d]
        doc = doc + (end <= places).astype(jnp.int32)
    return doc


def slot_targets(matrix_ref):
    first = chunk_in_group() * GROUP
    matrix = matrix_ref[...].astype(F32).astype(BF16)
    owner = iota((8, OWNERS), 1)
    nth = iota((8, OWNERS), 0)
    one = ((owner == first + nth) & (nth < GROUP)).astype(F32).astype(BF16)
    upto = ((owner >= first) & (owner <= first + nth) & (nth < GROUP)).astype(F32).astype(BF16)
    counts = dot(one, matrix, ((1,), (1,)))
    ends = dot(upto, matrix, ((1,), (1,)))
    earlier = (iota((OWNERS, OWNERS), 0) < iota((OWNERS, OWNERS), 1)).astype(F32).astype(BF16)
    arrive = dot(counts.astype(BF16), earlier)
    slots = OWNERS * CAP
    loader = iota((OWNERS, slots), 0)
    nth = (loader & 3) * 16 + (loader & 12) + lax.shift_right_logical(loader, 4)
    expand = (lax.shift_right_logical(iota((OWNERS, slots), 1), 4) == nth).astype(F32).astype(BF16)
    wide = dot(jnp.concatenate([counts, ends, arrive], axis=0).astype(BF16), expand)
    counts, ends, arrive = wide[:8], wide[8:16], wide[16:]
    slot = (iota((8, slots), 1) & (CAP - 1)).astype(F32)
    inside = (slot < ends) & (slot >= ends - counts)
    target = iota((8, slots), 0).astype(F32) * TOK + arrive + slot - (ends - counts) + 1.0
    return jnp.sum(jnp.where(inside, target, 0.0), axis=0, keepdims=True).astype(jnp.int32) - 1


def picked(targets):
    return (iota((CHUNK, OWNERS * CAP), 0) == targets).astype(F32).astype(BF16)


def place_kernel(matrix_ref, targets_ref, pick_ref):
    targets_ref[...] = slot_targets(matrix_ref)
    pick_ref[...] = picked(targets_ref[...])


def unpack(pick, received):
    return dot(pick, received.reshape(OWNERS * CAP, received.shape[2])).astype(BF16)


def column(row):
    return jnp.transpose(jnp.broadcast_to(row, (DK, DK)))


def decays(rate):
    rate = jnp.concatenate([rate[i * TOK : (i + 1) * TOK] for i in range(GROUP)], axis=1)
    tril = (iota((TOK, TOK), 0) >= iota((TOK, TOK), 1)).astype(F32).astype(BF16)
    high, middle, low = split(-jnp.exp(rate.astype(F32)))
    cumulative = dot(tril, high) + (dot(tril, middle) + dot(tril, low))
    parts = [cumulative[:, i * DK : (i + 1) * DK] for i in range(GROUP)]
    return [(part, part[TOK - 1 :, :]) for part in parts]


def doc_at(lengths_ref, place):
    return doc_of(lengths_ref, jnp.full((1, 1), place, jnp.int32))


def maps_kernel(lengths_ref, pick_ref, received_ref, rows_ref, map_ref):
    rows_ref[...] = unpack(pick_ref[...], received_ref[:, :, :LATE])
    first = chunk_start()
    parts = decays(rows_ref[:, DK : 2 * DK])
    after = jnp.zeros((1, DK), F32)
    end_keys = []
    for block in reversed(range(GROUP)):
        cumulative, whole = parts[block]
        key = rows_ref[block * TOK : (block + 1) * TOK, :DK].astype(F32)
        end_keys.insert(0, key * jnp.exp(whole - cumulative + after))
        after = after + whole
    doc_last = doc_at(lengths_ref, first + CHUNK - 1)
    doc_rows = doc_of(lengths_ref, first + iota((CHUNK, DK), 0))
    end_key = jnp.where(doc_rows == doc_last, jnp.concatenate(end_keys, axis=0), 0.0)
    state = dot_left(end_key, rows_ref[:, 2 * DK :], ((0,), (0,)))
    kept = column(jnp.where(doc_last == doc_at(lengths_ref, first - 1), jnp.exp(after), 0.0))
    half = DK // 2
    map_ref[:, 0, :DV] = state[:half]
    map_ref[:, 0, DV : 2 * DV] = state[half:]
    map_ref[:, 0, 2 * DV :] = jnp.where(iota((half, DK), 1) < half, kept[:half], kept[half:])


def block_kernel(lengths_ref, targets_ref, received_ref, rows_ref, partial_ref, query_out_ref):
    first = chunk_start()
    queries = unpack(picked(targets_ref[...]), received_ref[:, :, LATE:])
    state = None
    passed = jnp.zeros((1, DK), F32)
    chunk_before = doc_at(lengths_ref, first - 1)
    for block, (cumulative, whole) in enumerate(decays(rows_ref[:, DK : 2 * DK])):
        span = slice(block * TOK, (block + 1) * TOK)
        query = queries[span].astype(F32)
        key = rows_ref[span, :DK].astype(F32)
        value = rows_ref[span, 2 * DK :]
        start = first + block * TOK
        doc_rows = doc_of(lengths_ref, start + iota((TOK, DK), 0))
        doc_columns = doc_of(lengths_ref, start + iota((TOK, TOK), 1))
        doc_before = doc_at(lengths_ref, start - 1)
        doc_last = doc_at(lengths_ref, start + TOK - 1)
        half = 0.5 * whole
        scores = dot(
            query * jnp.exp(cumulative - half),
            key * jnp.exp(half - cumulative),
            ((1,), (1,)),
            PRECISE,
        )
        allowed = (iota((TOK, TOK), 0) >= iota((TOK, TOK), 1)) & (doc_rows == doc_columns)
        out = dot_left(jnp.where(allowed, scores, 0.0), value)
        if block > 0:
            kept = jnp.where(doc_rows == doc_before, query * jnp.exp(cumulative), 0.0)
            out = out + dot(kept, state, precision=PRECISE)
        partial_ref[span, :] = out
        query_out_ref[span, :] = jnp.where(
            doc_rows == chunk_before, query * jnp.exp(cumulative + passed), 0.0
        )
        if block < GROUP - 1:
            end_key = jnp.where(doc_rows == doc_last, key * jnp.exp(whole - cumulative), 0.0)
            fresh = dot_left(end_key, value, ((0,), (0,)))
            if block == 0:
                state = fresh
            else:
                kept = column(jnp.where(doc_last == doc_before, jnp.exp(whole), 0.0))
                state = jnp.concatenate([kept, kept], axis=1) * state + fresh
        passed = passed + whole


def scan_kernel(map_ref, prefix_ref):
    rows = map_ref.shape[0] // GROUP
    low = iota((rows, DK), 1) < DK // 2
    state = jnp.zeros((rows, 2 * DV), F32)
    kept = jnp.ones((rows, 2 * DV), F32)
    inside = []
    for nth in range(GROUP):
        inside.append((kept, state))
        here = map_ref[nth * rows : (nth + 1) * rows, 0, :]
        own = here[:, 2 * DV :]
        other = pltpu.roll(own, DK // 2, 1)
        one, two = jnp.where(low, own, other), jnp.where(low, other, own)
        own = jnp.concatenate([one, one, two, two], axis=1)
        state = own * state + here[:, : 2 * DV]
        kept = own * kept
    row = iota((rows, 2 * DV), 0)
    step = 1
    while step < rows:
        state = kept * jnp.where(row < step, 0.0, pltpu.roll(state, step, 0)) + state
        kept = kept * jnp.where(row < step, 1.0, pltpu.roll(kept, step, 0))
        step *= 2
    before = jnp.where(row < 1, 0.0, pltpu.roll(state, 1, 0))
    for nth, (kept, state) in enumerate(inside):
        prefix_ref[nth * rows : (nth + 1) * rows, 0, :] = kept * before + state


def finish_kernel(prefix_ref, partial_ref, query_ref, gain_ref, *out_refs):
    state = jnp.concatenate([prefix_ref[:, 0, :DV], prefix_ref[:, 0, DV:]], axis=0)
    head = lax.axis_index("zh")
    gain = gain_ref[pl.ds(head, 1), :]
    for turn, out_ref in enumerate(out_refs):
        span = pl.ds(pl.multiple_of(((head + turn) & 3) * TOK, TOK), TOK)
        mixed = partial_ref[span, :] + dot(query_ref[span, :], state, precision=PRECISE)
        scale = lax.rsqrt(jnp.mean(mixed * mixed, axis=1, keepdims=True) + EPSILON)
        out_ref[...] = (mixed * scale * gain).astype(BF16)


def join_kernel(*refs):
    for turn, ref in enumerate(refs[:-1]):
        head = (lax.axis_index("zl") - turn) & 3
        refs[-1][:, pl.ds(pl.multiple_of(head * DV, DV), DV)] = ref[...]


SMEM = pl.BlockSpec(memory_space=pltpu.SMEM)
VMEM = pl.BlockSpec(memory_space=pltpu.VMEM)
HBM = pl.BlockSpec(memory_space=pltpu.HBM)


def call(kernel, specs, outs, cost=0, scratch=(), limit=32 << 20):
    return pl.pallas_call(
        kernel,
        out_shape=outs,
        in_specs=specs,
        out_specs=jax.tree.map(lambda _: VMEM, outs),
        scratch_shapes=scratch,
        compiler_params=pltpu.CompilerParams(vmem_limit_bytes=limit),
        cost_estimate=pl.CostEstimate(flops=cost, bytes_accessed=1 << 20, transcendentals=0),
    )


def shape(dims, dtype=F32):
    return jax.ShapeDtypeStruct(dims, dtype)


def local(queries, key_vectors, value_vectors, decay_log, assignment, doc_lengths, norm_gain):
    matrix = assignment[0]
    streams = (matrix, queries[0], key_vectors[0], value_vectors[0], decay_log[0])
    packed = call(
        pack_kernel,
        [HBM] * 5,
        shape((4, HEADS, 4, CAP, WIDTH), BF16),
        1 << 28,
        [pltpu.VMEM(a.shape, a.dtype) for a in streams] + [pltpu.SemaphoreType.DMA((5,))],
        65500000,
    )(*streams)
    received = lax.all_to_all(packed.reshape(OWNERS, CAP, WIDTH), REGROUP, 0, 0, tiled=True)
    targets, pick = call(
        place_kernel,
        [VMEM],
        (shape((1, OWNERS * CAP), jnp.int32), shape((CHUNK, OWNERS * CAP), BF16)),
        1 << 28,
    )(matrix)
    rows, maps = call(
        maps_kernel,
        [SMEM, VMEM, VMEM],
        (shape((CHUNK, LATE), BF16), shape((OWNERS, 1, 2 * DV + DK))),
        1 << 29,
    )(doc_lengths, pick, received)
    maps = lax.all_to_all(maps, CHUNKS, 0, 0, tiled=True)
    partial, query = call(
        block_kernel,
        [SMEM, VMEM, VMEM, VMEM],
        (shape((CHUNK, DV)), shape((CHUNK, DK))),
        1 << 30,
    )(doc_lengths, targets, received, rows)
    prefix = call(scan_kernel, [VMEM], shape((OWNERS, 1, 2 * DV)), 1 << 24)(maps)
    prefix = lax.all_to_all(prefix, CHUNKS, 0, 0, tiled=True)
    parts = call(finish_kernel, [VMEM] * 4, [shape((TOK, DV), BF16)] * GROUP, 1 << 28)(
        prefix, partial, query, norm_gain.reshape(HEADS, DV)
    )
    pairs = [(head, nth) for head in range(HEADS) for nth in range(GROUP)]
    parts = [
        lax.ppermute(
            part, ("zh", "zl"), [(h * 4 + nth, nth * 4 + (h + turn) % 4) for h, nth in pairs]
        )
        for turn, part in enumerate(parts)
    ]
    out = call(join_kernel, [VMEM] * GROUP, shape((TOK, HEADS * DV), BF16))(*parts)
    return out.reshape(1, TOK, HEADS * DV)


def solution(mesh):
    split = Mesh(mesh.devices.reshape(4, 4, 4, 4, 2), ("y", "zh", "zl", "node", "tp"))
    rows = P("node", CTX, "tp")
    return jax.shard_map(
        local,
        mesh=split,
        in_specs=(rows, rows, rows, rows, P("node", None, None), P(), P("tp")),
        out_specs=rows,
        check_vma=False,
    )
```

```python
import jax
import jax.numpy as jnp
from jax import lax
from jax.experimental import pallas as pl
from jax.experimental.pallas import tpu as pltpu
from jax.sharding import Mesh, PartitionSpec as P

DK = 128
DV = 256
HEADS = 4
GROUP = 4
TOK = 128
CAP = 16
CHUNK = GROUP * TOK
OWNERS = 64
LATE = 2 * DK + DV
WIDTH = LATE + DK
EPSILON = 1e-05
CTX = ("y", "zh", "zl")
REGROUP = ("y", "zh", "zl")
CHUNKS = ("zl", "node", "y")
PRECISE = lax.Precision.HIGHEST
F32 = jnp.float32
BF16 = jnp.bfloat16


def iota(shape, dim):
    return lax.broadcasted_iota(jnp.int32, shape, dim)


def dot(a, b, dims=((1,), (0,)), precision=None):
    return lax.dot_general(a, b, (dims, ((), ())), precision=precision, preferred_element_type=F32)


def split(a):
    high = a.astype(BF16)
    rest = a - high.astype(F32)
    middle = rest.astype(BF16)
    return high, middle, (rest - middle.astype(F32)).astype(BF16)


def dot_left(a, b, dims=((1,), (0,))):
    high, middle, low = split(a)
    return dot(high, b, dims) + (dot(middle, b, dims) + dot(low, b, dims))


def pack_kernel(
    matrix_hbm, query_hbm, key_hbm, value_hbm, rate_hbm, out_ref,
    matrix_ref, query_ref, key_ref, value_ref, rate_ref, sems,
):
    sources = (matrix_hbm, key_hbm, rate_hbm, value_hbm, query_hbm)
    targets = (matrix_ref, key_ref, rate_ref, value_ref, query_ref)
    copies = [pltpu.make_async_copy(a, b, sems.at[i]) for i, (a, b) in enumerate(zip(sources, targets))]
    for copy in copies:
        copy.start()
    copies[0].wait()
    slots = (OWNERS // GROUP) * CAP
    counts = matrix_ref[pl.ds(lax.axis_index(CTX), 1), :].astype(F32)
    nth = lax.shift_right_logical(iota((slots, OWNERS), 0), 4)
    chunk = nth
    before = iota((slots, OWNERS), 1) < chunk * GROUP
    start = jnp.sum(jnp.where(before, counts, 0.0), axis=1, keepdims=True).astype(jnp.int32)
    wanted = start + (iota((slots, 1), 0) & (CAP - 1))
    pick = (iota((slots, TOK), 1) == wanted).astype(F32).astype(BF16)
    at = 0
    for copy, ref, width in zip(copies[1:], targets[1:], (DK, DK, DV, DK)):
        copy.wait()
        rows = dot(pick, ref[...]).astype(BF16)
        for head in range(HEADS):
            piece = rows[:, head * width : (head + 1) * width]
            out_ref[:, head, :, :, at : at + width] = piece.reshape(4, 4, CAP, width)
        at += width


def chunk_in_group():
    return lax.axis_index("y") * 4 + lax.axis_index("zl")


def chunk_start():
    return (lax.axis_index("node") * (OWNERS // GROUP) + chunk_in_group()) * CHUNK


def doc_of(lengths_ref, places):
    end = jnp.int32(0)
    doc = jnp.zeros_like(places)
    for d in range(lengths_ref.shape[0]):
        end = end + lengths_ref[d]
        doc = doc + (end <= places).astype(jnp.int32)
    return doc


def slot_targets(matrix_ref):
    first = chunk_in_group() * GROUP
    matrix = matrix_ref[...].astype(F32).astype(BF16)
    owner = iota((8, OWNERS), 1)
    nth = iota((8, OWNERS), 0)
    one = ((owner == first + nth) & (nth < GROUP)).astype(F32).astype(BF16)
    upto = ((owner >= first) & (owner <= first + nth) & (nth < GROUP)).astype(F32).astype(BF16)
    counts = dot(one, matrix, ((1,), (1,)))
    ends = dot(upto, matrix, ((1,), (1,)))
    earlier = (iota((OWNERS, OWNERS), 0) < iota((OWNERS, OWNERS), 1)).astype(F32).astype(BF16)
    arrive = dot(counts.astype(BF16), earlier)
    slots = OWNERS * CAP
    nth = iota((OWNERS, slots), 0)
    expand = (lax.shift_right_logical(iota((OWNERS, slots), 1), 4) == nth).astype(F32).astype(BF16)
    wide = dot(jnp.concatenate([counts, ends, arrive], axis=0).astype(BF16), expand)
    counts, ends, arrive = wide[:8], wide[8:16], wide[16:]
    slot = (iota((8, slots), 1) & (CAP - 1)).astype(F32)
    inside = (slot < ends) & (slot >= ends - counts)
    target = iota((8, slots), 0).astype(F32) * TOK + arrive + slot - (ends - counts) + 1.0
    return jnp.sum(jnp.where(inside, target, 0.0), axis=0, keepdims=True).astype(jnp.int32) - 1


def picked(targets):
    return (iota((CHUNK, OWNERS * CAP), 0) == targets).astype(F32).astype(BF16)


def place_kernel(matrix_ref, targets_ref, pick_ref):
    targets_ref[...] = slot_targets(matrix_ref)
    pick_ref[...] = picked(targets_ref[...])


def unpack(pick, received):
    return dot(pick, received.reshape(OWNERS * CAP, received.shape[2])).astype(BF16)


def column(row):
    return jnp.transpose(jnp.broadcast_to(row, (DK, DK)))


def decays(rate):
    rate = jnp.concatenate([rate[i * TOK : (i + 1) * TOK] for i in range(GROUP)], axis=1)
    tril = (iota((TOK, TOK), 0) >= iota((TOK, TOK), 1)).astype(F32).astype(BF16)
    high, middle, low = split(-jnp.exp(rate.astype(F32)))
    cumulative = dot(tril, high) + (dot(tril, middle) + dot(tril, low))
    parts = [cumulative[:, i * DK : (i + 1) * DK] for i in range(GROUP)]
    return [(part, part[TOK - 1 :, :]) for part in parts]


def doc_at(lengths_ref, place):
    return doc_of(lengths_ref, jnp.full((1, 1), place, jnp.int32))


def maps_kernel(lengths_ref, pick_ref, received_ref, rows_ref, map_ref):
    rows_ref[...] = unpack(pick_ref[...], received_ref[:, :, :LATE])
    first = chunk_start()
    parts = decays(rows_ref[:, DK : 2 * DK])
    after = jnp.zeros((1, DK), F32)
    end_keys = []
    for block in reversed(range(GROUP)):
        cumulative, whole = parts[block]
        key = rows_ref[block * TOK : (block + 1) * TOK, :DK].astype(F32)
        end_keys.insert(0, key * jnp.exp(whole - cumulative + after))
        after = after + whole
    doc_last = doc_at(lengths_ref, first + CHUNK - 1)
    doc_rows = doc_of(lengths_ref, first + iota((CHUNK, DK), 0))
    end_key = jnp.where(doc_rows == doc_last, jnp.concatenate(end_keys, axis=0), 0.0)
    state = dot_left(end_key, rows_ref[:, 2 * DK :], ((0,), (0,)))
    kept = column(jnp.where(doc_last == doc_at(lengths_ref, first - 1), jnp.exp(after), 0.0))
    half = DK // 2
    map_ref[:, 0, :DV] = state[:half]
    map_ref[:, 0, DV : 2 * DV] = state[half:]
    map_ref[:, 0, 2 * DV :] = jnp.where(iota((half, DK), 1) < half, kept[:half], kept[half:])


def block_kernel(lengths_ref, targets_ref, received_ref, rows_ref, partial_ref, query_out_ref):
    first = chunk_start()
    queries = unpack(picked(targets_ref[...]), received_ref[:, :, LATE:])
    state = None
    passed = jnp.zeros((1, DK), F32)
    chunk_before = doc_at(lengths_ref, first - 1)
    for block, (cumulative, whole) in enumerate(decays(rows_ref[:, DK : 2 * DK])):
        span = slice(block * TOK, (block + 1) * TOK)
        query = queries[span].astype(F32)
        key = rows_ref[span, :DK].astype(F32)
        value = rows_ref[span, 2 * DK :]
        start = first + block * TOK
        doc_rows = doc_of(lengths_ref, start + iota((TOK, DK), 0))
        doc_columns = doc_of(lengths_ref, start + iota((TOK, TOK), 1))
        doc_before = doc_at(lengths_ref, start - 1)
        doc_last = doc_at(lengths_ref, start + TOK - 1)
        half = 0.5 * whole
        scores = dot(
            query * jnp.exp(cumulative - half),
            key * jnp.exp(half - cumulative),
            ((1,), (1,)),
            PRECISE,
        )
        allowed = (iota((TOK, TOK), 0) >= iota((TOK, TOK), 1)) & (doc_rows == doc_columns)
        out = dot_left(jnp.where(allowed, scores, 0.0), value)
        if block > 0:
            kept = jnp.where(doc_rows == doc_before, query * jnp.exp(cumulative), 0.0)
            out = out + dot(kept, state, precision=PRECISE)
        partial_ref[span, :] = out
        query_out_ref[span, :] = jnp.where(
            doc_rows == chunk_before, query * jnp.exp(cumulative + passed), 0.0
        )
        if block < GROUP - 1:
            end_key = jnp.where(doc_rows == doc_last, key * jnp.exp(whole - cumulative), 0.0)
            fresh = dot_left(end_key, value, ((0,), (0,)))
            if block == 0:
                state = fresh
            else:
                kept = column(jnp.where(doc_last == doc_before, jnp.exp(whole), 0.0))
                state = jnp.concatenate([kept, kept], axis=1) * state + fresh
        passed = passed + whole


def scan_kernel(map_ref, prefix_ref):
    rows = map_ref.shape[0] // GROUP
    low = iota((rows, DK), 1) < DK // 2
    state = jnp.zeros((rows, 2 * DV), F32)
    kept = jnp.ones((rows, 2 * DV), F32)
    inside = []
    for nth in range(GROUP):
        inside.append((kept, state))
        here = map_ref[nth * rows : (nth + 1) * rows, 0, :]
        own = here[:, 2 * DV :]
        other = pltpu.roll(own, DK // 2, 1)
        one, two = jnp.where(low, own, other), jnp.where(low, other, own)
        own = jnp.concatenate([one, one, two, two], axis=1)
        state = own * state + here[:, : 2 * DV]
        kept = own * kept
    row = iota((rows, 2 * DV), 0)
    step = 1
    while step < rows:
        state = kept * jnp.where(row < step, 0.0, pltpu.roll(state, step, 0)) + state
        kept = kept * jnp.where(row < step, 1.0, pltpu.roll(kept, step, 0))
        step *= 2
    before = jnp.where(row < 1, 0.0, pltpu.roll(state, 1, 0))
    for nth, (kept, state) in enumerate(inside):
        prefix_ref[nth * rows : (nth + 1) * rows, 0, :] = kept * before + state


def finish_kernel(prefix_ref, partial_ref, query_ref, gain_ref, *out_refs):
    state = jnp.concatenate([prefix_ref[:, 0, :DV], prefix_ref[:, 0, DV:]], axis=0)
    head = lax.axis_index("zh")
    gain = gain_ref[pl.ds(head, 1), :]
    for turn, out_ref in enumerate(out_refs):
        span = pl.ds(pl.multiple_of(((head + turn) & 3) * TOK, TOK), TOK)
        mixed = partial_ref[span, :] + dot(query_ref[span, :], state, precision=PRECISE)
        scale = lax.rsqrt(jnp.mean(mixed * mixed, axis=1, keepdims=True) + EPSILON)
        out_ref[...] = (mixed * scale * gain).astype(BF16)


def join_kernel(*refs):
    for turn, ref in enumerate(refs[:-1]):
        head = (lax.axis_index("zl") - turn) & 3
        refs[-1][:, pl.ds(pl.multiple_of(head * DV, DV), DV)] = ref[...]


SMEM = pl.BlockSpec(memory_space=pltpu.SMEM)
VMEM = pl.BlockSpec(memory_space=pltpu.VMEM)
HBM = pl.BlockSpec(memory_space=pltpu.HBM)


def call(kernel, specs, outs, cost=0, scratch=(), limit=32 << 20):
    return pl.pallas_call(
        kernel,
        out_shape=outs,
        in_specs=specs,
        out_specs=jax.tree.map(lambda _: VMEM, outs),
        scratch_shapes=scratch,
        compiler_params=pltpu.CompilerParams(vmem_limit_bytes=limit),
        cost_estimate=pl.CostEstimate(flops=cost, bytes_accessed=1 << 20, transcendentals=0),
    )


def shape(dims, dtype=F32):
    return jax.ShapeDtypeStruct(dims, dtype)


def local(queries, key_vectors, value_vectors, decay_log, assignment, doc_lengths, norm_gain):
    matrix = assignment[0]
    streams = (matrix, queries[0], key_vectors[0], value_vectors[0], decay_log[0])
    packed = call(
        pack_kernel,
        [HBM] * 5,
        shape((4, HEADS, 4, CAP, WIDTH), BF16),
        1 << 28,
        [pltpu.VMEM(a.shape, a.dtype) for a in streams] + [pltpu.SemaphoreType.DMA((5,))],
        65500000,
    )(*streams)
    received = lax.all_to_all(packed.reshape(OWNERS, CAP, WIDTH), REGROUP, 0, 0, tiled=True)
    targets, pick = call(
        place_kernel,
        [VMEM],
        (shape((1, OWNERS * CAP), jnp.int32), shape((CHUNK, OWNERS * CAP), BF16)),
        1 << 28,
    )(matrix)
    rows, maps = call(
        maps_kernel,
        [SMEM, VMEM, VMEM],
        (shape((CHUNK, LATE), BF16), shape((OWNERS, 1, 2 * DV + DK))),
        1 << 29,
    )(doc_lengths, pick, received)
    maps = lax.all_to_all(maps, CHUNKS, 0, 0, tiled=True)
    partial, query = call(
        block_kernel,
        [SMEM, VMEM, VMEM, VMEM],
        (shape((CHUNK, DV)), shape((CHUNK, DK))),
        1 << 30,
    )(doc_lengths, targets, received, rows)
    prefix = call(scan_kernel, [VMEM], shape((OWNERS, 1, 2 * DV)), 1 << 24)(maps)
    prefix = lax.all_to_all(prefix, CHUNKS, 0, 0, tiled=True)
    parts = call(finish_kernel, [VMEM] * 4, [shape((TOK, DV), BF16)] * GROUP, 1 << 28)(
        prefix, partial, query, norm_gain.reshape(HEADS, DV)
    )
    pairs = [(head, nth) for head in range(HEADS) for nth in range(GROUP)]
    parts = [
        lax.ppermute(
            part, ("zh", "zl"), [(h * 4 + nth, nth * 4 + (h + turn) % 4) for h, nth in pairs]
        )
        for turn, part in enumerate(parts)
    ]
    out = call(join_kernel, [VMEM] * GROUP, shape((TOK, HEADS * DV), BF16))(*parts)
    return out.reshape(1, TOK, HEADS * DV)


def solution(mesh):
    split = Mesh(mesh.devices.reshape(4, 4, 4, 4, 2), ("y", "zh", "zl", "node", "tp"))
    rows = P("node", CTX, "tp")
    return jax.shard_map(
        local,
        mesh=split,
        in_specs=(rows, rows, rows, rows, P("node", None, None), P(), P("tp")),
        out_specs=rows,
        check_vma=False,
    )
```

```python
import jax
import jax.numpy as jnp
from jax import lax
from jax.experimental import pallas as pl
from jax.experimental.pallas import tpu as pltpu
from jax.sharding import Mesh, PartitionSpec as P

DK = 128
DV = 256
TURN = (3, 0, 2, 1)
HEADS = 4
GROUP = 4
TOK = 128
CAP = 16
CHUNK = GROUP * TOK
OWNERS = 64
LATE = 2 * DK + DV
WIDTH = LATE + DK
EPSILON = 1e-05
CTX = ("y", "zh", "zl")
REGROUP = ("y", "zh", "zl")
CHUNKS = ("zl", "node", "y")
PRECISE = lax.Precision.HIGHEST
F32 = jnp.float32
BF16 = jnp.bfloat16


def iota(shape, dim):
    return lax.broadcasted_iota(jnp.int32, shape, dim)


def dot(a, b, dims=((1,), (0,)), precision=None):
    return lax.dot_general(a, b, (dims, ((), ())), precision=precision, preferred_element_type=F32)


def split(a):
    high = a.astype(BF16)
    rest = a - high.astype(F32)
    middle = rest.astype(BF16)
    return high, middle, (rest - middle.astype(F32)).astype(BF16)


def dot_left(a, b, dims=((1,), (0,))):
    high, middle, low = split(a)
    return dot(high, b, dims) + (dot(middle, b, dims) + dot(low, b, dims))


def pack_kernel(
    matrix_hbm, query_hbm, key_hbm, value_hbm, rate_hbm, out_hbm,
    matrix_ref, query_ref, key_ref, value_ref, rate_ref, out_ref, sems, out_sems,
):
    sources = (matrix_hbm, key_hbm, rate_hbm, value_hbm, query_hbm)
    targets = (matrix_ref, key_ref, rate_ref, value_ref, query_ref)
    copies = [pltpu.make_async_copy(a, b, sems.at[i]) for i, (a, b) in enumerate(zip(sources, targets))]
    for copy in copies:
        copy.start()
    copies[0].wait()
    slots = (OWNERS // GROUP) * CAP
    counts = matrix_ref[pl.ds(lax.axis_index(CTX), 1), :].astype(F32)
    nth = lax.shift_right_logical(iota((slots, OWNERS), 0), 4)
    chunk = nth
    before = iota((slots, OWNERS), 1) < chunk * GROUP
    start = jnp.sum(jnp.where(before, counts, 0.0), axis=1, keepdims=True).astype(jnp.int32)
    wanted = start + (iota((slots, 1), 0) & (CAP - 1))
    pick = (iota((slots, TOK), 1) == wanted).astype(F32).astype(BF16)
    at = 0
    leaving = []
    for copy, ref, width in zip(copies[1:], targets[1:], (DK, DK, DV, DK)):
        copy.wait()
        rows = dot(pick, ref[...]).astype(BF16)
        for head in range(HEADS):
            piece = rows[:, head * width : (head + 1) * width]
            piece = piece.reshape(4, 4, CAP, width)
            for nth, turn in enumerate(TURN):
                out_ref[:, head, nth, :, at : at + width] = piece[:, (head + turn) % 4]
        columns = pl.ds(at, width)
        leaving.append(
            pltpu.make_async_copy(
                out_ref.at[:, :, :, :, columns],
                out_hbm.at[:, :, :, :, columns],
                out_sems.at[len(leaving)],
            )
        )
        leaving[-1].start()
        at += width
    for copy in leaving:
        copy.wait()


def chunk_in_group():
    nth = lax.axis_index("zl")
    turn = sum([jnp.where(nth == i, turn, 0) for i, turn in enumerate(TURN)])
    return lax.axis_index("y") * 4 + ((lax.axis_index("zh") + turn) & 3)


def chunk_start():
    return (lax.axis_index("node") * (OWNERS // GROUP) + chunk_in_group()) * CHUNK


def doc_of(lengths_ref, places):
    end = jnp.int32(0)
    doc = jnp.zeros_like(places)
    for d in range(lengths_ref.shape[0]):
        end = end + lengths_ref[d]
        doc = doc + (end <= places).astype(jnp.int32)
    return doc


def slot_targets(matrix_ref):
    first = chunk_in_group() * GROUP
    matrix = matrix_ref[...].astype(F32).astype(BF16)
    owner = iota((8, OWNERS), 1)
    nth = iota((8, OWNERS), 0)
    one = ((owner == first + nth) & (nth < GROUP)).astype(F32).astype(BF16)
    upto = ((owner >= first) & (owner <= first + nth) & (nth < GROUP)).astype(F32).astype(BF16)
    counts = dot(one, matrix, ((1,), (1,)))
    ends = dot(upto, matrix, ((1,), (1,)))
    earlier = (iota((OWNERS, OWNERS), 0) < iota((OWNERS, OWNERS), 1)).astype(F32).astype(BF16)
    arrive = dot(counts.astype(BF16), earlier)
    slots = OWNERS * CAP
    nth = iota((OWNERS, slots), 0)
    expand = (lax.shift_right_logical(iota((OWNERS, slots), 1), 4) == nth).astype(F32).astype(BF16)
    wide = dot(jnp.concatenate([counts, ends, arrive], axis=0).astype(BF16), expand)
    counts, ends, arrive = wide[:8], wide[8:16], wide[16:]
    slot = (iota((8, slots), 1) & (CAP - 1)).astype(F32)
    inside = (slot < ends) & (slot >= ends - counts)
    target = iota((8, slots), 0).astype(F32) * TOK + arrive + slot - (ends - counts) + 1.0
    return jnp.sum(jnp.where(inside, target, 0.0), axis=0, keepdims=True).astype(jnp.int32) - 1


def picked(targets):
    return (iota((CHUNK, OWNERS * CAP), 0) == targets).astype(F32).astype(BF16)


def place_kernel(matrix_ref, targets_ref, pick_ref):
    targets_ref[...] = slot_targets(matrix_ref)
    pick_ref[...] = picked(targets_ref[...])


def unpack(pick, received):
    return dot(pick, received.reshape(OWNERS * CAP, received.shape[2])).astype(BF16)


def column(row):
    return jnp.transpose(jnp.broadcast_to(row, (DK, DK)))


def decays(rate):
    rate = jnp.concatenate([rate[i * TOK : (i + 1) * TOK] for i in range(GROUP)], axis=1)
    tril = (iota((TOK, TOK), 0) >= iota((TOK, TOK), 1)).astype(F32).astype(BF16)
    high, middle, low = split(-jnp.exp(rate.astype(F32)))
    cumulative = dot(tril, high) + (dot(tril, middle) + dot(tril, low))
    parts = [cumulative[:, i * DK : (i + 1) * DK] for i in range(GROUP)]
    return [(part, part[TOK - 1 :, :]) for part in parts]


def doc_at(lengths_ref, place):
    return doc_of(lengths_ref, jnp.full((1, 1), place, jnp.int32))


def maps_kernel(lengths_ref, pick_ref, received_ref, rows_ref, map_ref):
    rows_ref[...] = unpack(pick_ref[...], received_ref[:, :, :LATE])
    first = chunk_start()
    parts = decays(rows_ref[:, DK : 2 * DK])
    after = jnp.zeros((1, DK), F32)
    end_keys = []
    for block in reversed(range(GROUP)):
        cumulative, whole = parts[block]
        key = rows_ref[block * TOK : (block + 1) * TOK, :DK].astype(F32)
        end_keys.insert(0, key * jnp.exp(whole - cumulative + after))
        after = after + whole
    doc_last = doc_at(lengths_ref, first + CHUNK - 1)
    doc_rows = doc_of(lengths_ref, first + iota((CHUNK, DK), 0))
    end_key = jnp.where(doc_rows == doc_last, jnp.concatenate(end_keys, axis=0), 0.0)
    state = dot_left(end_key, rows_ref[:, 2 * DK :], ((0,), (0,)))
    kept = column(jnp.where(doc_last == doc_at(lengths_ref, first - 1), jnp.exp(after), 0.0))
    half = DK // 2
    map_ref[:, 0, :DV] = state[:half]
    map_ref[:, 0, DV : 2 * DV] = state[half:]
    map_ref[:, 0, 2 * DV :] = jnp.where(iota((half, DK), 1) < half, kept[:half], kept[half:])


def block_kernel(lengths_ref, targets_ref, received_ref, rows_ref, partial_ref, query_out_ref):
    first = chunk_start()
    queries = unpack(picked(targets_ref[...]), received_ref[:, :, LATE:])
    state = None
    passed = jnp.zeros((1, DK), F32)
    chunk_before = doc_at(lengths_ref, first - 1)
    for block, (cumulative, whole) in enumerate(decays(rows_ref[:, DK : 2 * DK])):
        span = slice(block * TOK, (block + 1) * TOK)
        query = queries[span].astype(F32)
        key = rows_ref[span, :DK].astype(F32)
        value = rows_ref[span, 2 * DK :]
        start = first + block * TOK
        doc_rows = doc_of(lengths_ref, start + iota((TOK, DK), 0))
        doc_columns = doc_of(lengths_ref, start + iota((TOK, TOK), 1))
        doc_before = doc_at(lengths_ref, start - 1)
        doc_last = doc_at(lengths_ref, start + TOK - 1)
        half = 0.5 * whole
        scores = dot(
            query * jnp.exp(cumulative - half),
            key * jnp.exp(half - cumulative),
            ((1,), (1,)),
            PRECISE,
        )
        allowed = (iota((TOK, TOK), 0) >= iota((TOK, TOK), 1)) & (doc_rows == doc_columns)
        out = dot_left(jnp.where(allowed, scores, 0.0), value)
        if block > 0:
            kept = jnp.where(doc_rows == doc_before, query * jnp.exp(cumulative), 0.0)
            out = out + dot(kept, state, precision=PRECISE)
        partial_ref[span, :] = out
        query_out_ref[span, :] = jnp.where(
            doc_rows == chunk_before, query * jnp.exp(cumulative + passed), 0.0
        )
        if block < GROUP - 1:
            end_key = jnp.where(doc_rows == doc_last, key * jnp.exp(whole - cumulative), 0.0)
            fresh = dot_left(end_key, value, ((0,), (0,)))
            if block == 0:
                state = fresh
            else:
                kept = column(jnp.where(doc_last == doc_before, jnp.exp(whole), 0.0))
                state = jnp.concatenate([kept, kept], axis=1) * state + fresh
        passed = passed + whole


def scan_kernel(map_ref, prefix_ref):
    rows = map_ref.shape[0] // GROUP
    low = iota((rows, DK), 1) < DK // 2
    state = jnp.zeros((rows, 2 * DV), F32)
    kept = jnp.ones((rows, 2 * DV), F32)
    inside = []
    for chunk in range(GROUP):
        turn = (chunk - lax.axis_index("zh")) & 3
        nth = sum([jnp.where(turn == a, i, 0) for i, a in enumerate(TURN)])
        span = pl.ds(nth * rows, rows)
        inside.append((span, kept, state))
        here = map_ref[span, 0, :]
        own = here[:, 2 * DV :]
        other = pltpu.roll(own, DK // 2, 1)
        one, two = jnp.where(low, own, other), jnp.where(low, other, own)
        own = jnp.concatenate([one, one, two, two], axis=1)
        state = own * state + here[:, : 2 * DV]
        kept = own * kept
    row = iota((rows, 2 * DV), 0)
    step = 1
    while step < rows:
        state = kept * jnp.where(row < step, 0.0, pltpu.roll(state, step, 0)) + state
        kept = kept * jnp.where(row < step, 1.0, pltpu.roll(kept, step, 0))
        step *= 2
    before = jnp.where(row < 1, 0.0, pltpu.roll(state, 1, 0))
    for span, kept, state in inside:
        prefix_ref[span, 0, :] = kept * before + state


def finish_kernel(prefix_ref, partial_ref, query_ref, gain_ref, *out_refs):
    state = jnp.concatenate([prefix_ref[:, 0, :DV], prefix_ref[:, 0, DV:]], axis=0)
    head = lax.axis_index("zh")
    gain = gain_ref[pl.ds(head, 1), :]
    for turn, out_ref in enumerate(out_refs):
        span = pl.ds(pl.multiple_of((head ^ turn) * TOK, TOK), TOK)
        mixed = partial_ref[span, :] + dot(query_ref[span, :], state, precision=PRECISE)
        scale = lax.rsqrt(jnp.mean(mixed * mixed, axis=1, keepdims=True) + EPSILON)
        out_ref[...] = (mixed * scale * gain).astype(BF16)


def join_kernel(*refs):
    for turn, ref in enumerate(refs[:-1]):
        head = lax.axis_index("zl") ^ turn
        refs[-1][:, pl.ds(pl.multiple_of(head * DV, DV), DV)] = ref[...]


SMEM = pl.BlockSpec(memory_space=pltpu.SMEM)
VMEM = pl.BlockSpec(memory_space=pltpu.VMEM)
HBM = pl.BlockSpec(memory_space=pltpu.HBM)


def call(kernel, specs, outs, cost=0, scratch=(), limit=32 << 20, out_spec=None):
    return pl.pallas_call(
        kernel,
        out_shape=outs,
        in_specs=specs,
        out_specs=jax.tree.map(lambda _: out_spec or VMEM, outs),
        scratch_shapes=scratch,
        compiler_params=pltpu.CompilerParams(vmem_limit_bytes=limit),
        cost_estimate=pl.CostEstimate(flops=cost, bytes_accessed=1 << 20, transcendentals=0),
    )


def shape(dims, dtype=F32):
    return jax.ShapeDtypeStruct(dims, dtype)


def local(queries, key_vectors, value_vectors, decay_log, assignment, doc_lengths, norm_gain):
    matrix = assignment[0]
    streams = (matrix, queries[0], key_vectors[0], value_vectors[0], decay_log[0])
    packed = call(
        pack_kernel,
        [HBM] * 5,
        shape((4, HEADS, 4, CAP, WIDTH), BF16),
        1 << 28,
        [pltpu.VMEM(a.shape, a.dtype) for a in streams]
        + [pltpu.VMEM((4, HEADS, 4, CAP, WIDTH), BF16)]
        + [pltpu.SemaphoreType.DMA((5,)), pltpu.SemaphoreType.DMA((4,))],
        65500000,
        HBM,
    )(*streams)
    received = lax.all_to_all(packed.reshape(OWNERS, CAP, WIDTH), REGROUP, 0, 0, tiled=True)
    targets, pick = call(
        place_kernel,
        [VMEM],
        (shape((1, OWNERS * CAP), jnp.int32), shape((CHUNK, OWNERS * CAP), BF16)),
        1 << 28,
    )(matrix)
    rows, maps = call(
        maps_kernel,
        [SMEM, VMEM, VMEM],
        (shape((CHUNK, LATE), BF16), shape((OWNERS, 1, 2 * DV + DK))),
        1 << 29,
    )(doc_lengths, pick, received)
    maps = lax.all_to_all(maps, CHUNKS, 0, 0, tiled=True)
    partial, query = call(
        block_kernel,
        [SMEM, VMEM, VMEM, VMEM],
        (shape((CHUNK, DV)), shape((CHUNK, DK))),
        1 << 30,
    )(doc_lengths, targets, received, rows)
    prefix = call(scan_kernel, [VMEM], shape((OWNERS, 1, 2 * DV)), 1 << 24)(maps)
    prefix = lax.all_to_all(prefix, CHUNKS, 0, 0, tiled=True)
    parts = call(finish_kernel, [VMEM] * 4, [shape((TOK, DV), BF16)] * GROUP, 1 << 28)(
        prefix, partial, query, norm_gain.reshape(HEADS, DV)
    )
    pairs = [(head, nth) for head in range(HEADS) for nth in range(GROUP)]
    parts = [
        lax.ppermute(
            part, ("zh", "zl"), [(h * 4 + n, (h + TURN[n]) % 4 * 4 + (h ^ turn)) for h, n in pairs]
        )
        for turn, part in enumerate(parts)
    ]
    out = call(join_kernel, [VMEM] * GROUP, shape((TOK, HEADS * DV), BF16))(*parts)
    return out.reshape(1, TOK, HEADS * DV)


def solution(mesh):
    split = Mesh(mesh.devices.reshape(4, 4, 4, 4, 2), ("y", "zh", "zl", "node", "tp"))
    rows = P("node", CTX, "tp")
    return jax.shard_map(
        local,
        mesh=split,
        in_specs=(rows, rows, rows, rows, P("node", None, None), P(), P("tp")),
        out_specs=rows,
        check_vma=False,
    )
```

```python
import jax
import jax.numpy as jnp
from jax import lax
from jax.experimental import pallas as pl
from jax.experimental.pallas import tpu as pltpu
from jax.sharding import Mesh, PartitionSpec as P

DK = 128
DV = 256
TURN = (3, 0, 2, 1)
HEADS = 4
GROUP = 4
TOK = 128
CAP = 16
CHUNK = GROUP * TOK
OWNERS = 64
LATE = 2 * DK + DV
WIDTH = LATE + DK
EPSILON = 1e-05
CTX = ("y", "zh", "zl")
REGROUP = ("y", "zh", "zl")
CHUNKS = ("node", "zl", "y")
PRECISE = lax.Precision.HIGHEST
F32 = jnp.float32
BF16 = jnp.bfloat16


def iota(shape, dim):
    return lax.broadcasted_iota(jnp.int32, shape, dim)


def dot(a, b, dims=((1,), (0,)), precision=None):
    return lax.dot_general(a, b, (dims, ((), ())), precision=precision, preferred_element_type=F32)


def split(a):
    high = a.astype(BF16)
    rest = a - high.astype(F32)
    middle = rest.astype(BF16)
    return high, middle, (rest - middle.astype(F32)).astype(BF16)


def dot_left(a, b, dims=((1,), (0,))):
    high, middle, low = split(a)
    return dot(high, b, dims) + (dot(middle, b, dims) + dot(low, b, dims))


def pack_kernel(
    matrix_hbm, query_hbm, key_hbm, value_hbm, rate_hbm, out_hbm,
    matrix_ref, query_ref, key_ref, value_ref, rate_ref, out_ref, sems, out_sems,
):
    sources = (matrix_hbm, key_hbm, rate_hbm, value_hbm, query_hbm)
    targets = (matrix_ref, key_ref, rate_ref, value_ref, query_ref)
    copies = [pltpu.make_async_copy(a, b, sems.at[i]) for i, (a, b) in enumerate(zip(sources, targets))]
    for copy in copies:
        copy.start()
    copies[0].wait()
    slots = (OWNERS // GROUP) * CAP
    counts = matrix_ref[pl.ds(lax.axis_index(CTX), 1), :].astype(F32)
    nth = lax.shift_right_logical(iota((slots, OWNERS), 0), 4)
    chunk = nth
    before = iota((slots, OWNERS), 1) < chunk * GROUP
    start = jnp.sum(jnp.where(before, counts, 0.0), axis=1, keepdims=True).astype(jnp.int32)
    wanted = start + (iota((slots, 1), 0) & (CAP - 1))
    pick = (iota((slots, TOK), 1) == wanted).astype(F32).astype(BF16)
    at = 0
    leaving = []
    for copy, ref, width in zip(copies[1:], targets[1:], (DK, DK, DV, DK)):
        copy.wait()
        rows = dot(pick, ref[...]).astype(BF16)
        for head in range(HEADS):
            piece = rows[:, head * width : (head + 1) * width]
            piece = piece.reshape(4, 4, CAP, width)
            for nth, turn in enumerate(TURN):
                out_ref[:, head, nth, :, at : at + width] = piece[:, (head + turn) % 4]
        columns = pl.ds(at, width)
        leaving.append(
            pltpu.make_async_copy(
                out_ref.at[:, :, :, :, columns],
                out_hbm.at[:, :, :, :, columns],
                out_sems.at[len(leaving)],
            )
        )
        leaving[-1].start()
        at += width
    for copy in leaving:
        copy.wait()


def chunk_in_group():
    nth = lax.axis_index("zl")
    turn = sum([jnp.where(nth == i, turn, 0) for i, turn in enumerate(TURN)])
    return lax.axis_index("y") * 4 + ((lax.axis_index("zh") + turn) & 3)


def chunk_start():
    return (lax.axis_index("node") * (OWNERS // GROUP) + chunk_in_group()) * CHUNK


def doc_of(lengths_ref, places):
    end = jnp.int32(0)
    doc = jnp.zeros_like(places)
    for d in range(lengths_ref.shape[0]):
        end = end + lengths_ref[d]
        doc = doc + (end <= places).astype(jnp.int32)
    return doc


def slot_targets(matrix_ref):
    first = chunk_in_group() * GROUP
    matrix = matrix_ref[...].astype(F32).astype(BF16)
    owner = iota((8, OWNERS), 1)
    nth = iota((8, OWNERS), 0)
    one = ((owner == first + nth) & (nth < GROUP)).astype(F32).astype(BF16)
    upto = ((owner >= first) & (owner <= first + nth) & (nth < GROUP)).astype(F32).astype(BF16)
    counts = dot(one, matrix, ((1,), (1,)))
    ends = dot(upto, matrix, ((1,), (1,)))
    earlier = (iota((OWNERS, OWNERS), 0) < iota((OWNERS, OWNERS), 1)).astype(F32).astype(BF16)
    arrive = dot(counts.astype(BF16), earlier)
    slots = OWNERS * CAP
    nth = iota((OWNERS, slots), 0)
    expand = (lax.shift_right_logical(iota((OWNERS, slots), 1), 4) == nth).astype(F32).astype(BF16)
    wide = dot(jnp.concatenate([counts, ends, arrive], axis=0).astype(BF16), expand)
    counts, ends, arrive = wide[:8], wide[8:16], wide[16:]
    slot = (iota((8, slots), 1) & (CAP - 1)).astype(F32)
    inside = (slot < ends) & (slot >= ends - counts)
    target = iota((8, slots), 0).astype(F32) * TOK + arrive + slot - (ends - counts) + 1.0
    return jnp.sum(jnp.where(inside, target, 0.0), axis=0, keepdims=True).astype(jnp.int32) - 1


def picked(targets):
    return (iota((CHUNK, OWNERS * CAP), 0) == targets).astype(F32).astype(BF16)


def place_kernel(matrix_ref, targets_ref, pick_ref):
    targets_ref[...] = slot_targets(matrix_ref)
    pick_ref[...] = picked(targets_ref[...])


def unpack(pick, received):
    return dot(pick, received.reshape(OWNERS * CAP, received.shape[2])).astype(BF16)


def column(row):
    return jnp.transpose(jnp.broadcast_to(row, (DK, DK)))


def decays(rate):
    rate = jnp.concatenate([rate[i * TOK : (i + 1) * TOK] for i in range(GROUP)], axis=1)
    tril = (iota((TOK, TOK), 0) >= iota((TOK, TOK), 1)).astype(F32).astype(BF16)
    high, middle, low = split(-jnp.exp(rate.astype(F32)))
    cumulative = dot(tril, high) + (dot(tril, middle) + dot(tril, low))
    parts = [cumulative[:, i * DK : (i + 1) * DK] for i in range(GROUP)]
    return [(part, part[TOK - 1 :, :]) for part in parts]


def doc_at(lengths_ref, place):
    return doc_of(lengths_ref, jnp.full((1, 1), place, jnp.int32))


def maps_kernel(lengths_ref, pick_ref, received_ref, rows_ref, map_ref):
    rows_ref[...] = unpack(pick_ref[...], received_ref[:, :, :LATE])
    first = chunk_start()
    parts = decays(rows_ref[:, DK : 2 * DK])
    after = jnp.zeros((1, DK), F32)
    end_keys = []
    for block in reversed(range(GROUP)):
        cumulative, whole = parts[block]
        key = rows_ref[block * TOK : (block + 1) * TOK, :DK].astype(F32)
        end_keys.insert(0, key * jnp.exp(whole - cumulative + after))
        after = after + whole
    doc_last = doc_at(lengths_ref, first + CHUNK - 1)
    doc_rows = doc_of(lengths_ref, first + iota((CHUNK, DK), 0))
    end_key = jnp.where(doc_rows == doc_last, jnp.concatenate(end_keys, axis=0), 0.0)
    state = dot_left(end_key, rows_ref[:, 2 * DK :], ((0,), (0,)))
    kept = column(jnp.where(doc_last == doc_at(lengths_ref, first - 1), jnp.exp(after), 0.0))
    half = DK // 2
    map_ref[:, 0, :DV] = state[:half]
    map_ref[:, 0, DV : 2 * DV] = state[half:]
    map_ref[:, 0, 2 * DV :] = jnp.where(iota((half, DK), 1) < half, kept[:half], kept[half:])


def block_kernel(lengths_ref, targets_ref, received_ref, rows_ref, partial_ref, query_out_ref):
    first = chunk_start()
    queries = unpack(picked(targets_ref[...]), received_ref[:, :, LATE:])
    state = None
    passed = jnp.zeros((1, DK), F32)
    chunk_before = doc_at(lengths_ref, first - 1)
    for block, (cumulative, whole) in enumerate(decays(rows_ref[:, DK : 2 * DK])):
        span = slice(block * TOK, (block + 1) * TOK)
        query = queries[span].astype(F32)
        key = rows_ref[span, :DK].astype(F32)
        value = rows_ref[span, 2 * DK :]
        start = first + block * TOK
        doc_rows = doc_of(lengths_ref, start + iota((TOK, DK), 0))
        doc_columns = doc_of(lengths_ref, start + iota((TOK, TOK), 1))
        doc_before = doc_at(lengths_ref, start - 1)
        doc_last = doc_at(lengths_ref, start + TOK - 1)
        half = 0.5 * whole
        scores = dot(
            query * jnp.exp(cumulative - half),
            key * jnp.exp(half - cumulative),
            ((1,), (1,)),
            PRECISE,
        )
        allowed = (iota((TOK, TOK), 0) >= iota((TOK, TOK), 1)) & (doc_rows == doc_columns)
        out = dot_left(jnp.where(allowed, scores, 0.0), value)
        if block > 0:
            kept = jnp.where(doc_rows == doc_before, query * jnp.exp(cumulative), 0.0)
            out = out + dot(kept, state, precision=PRECISE)
        partial_ref[span, :] = out
        query_out_ref[span, :] = jnp.where(
            doc_rows == chunk_before, query * jnp.exp(cumulative + passed), 0.0
        )
        if block < GROUP - 1:
            end_key = jnp.where(doc_rows == doc_last, key * jnp.exp(whole - cumulative), 0.0)
            fresh = dot_left(end_key, value, ((0,), (0,)))
            if block == 0:
                state = fresh
            else:
                kept = column(jnp.where(doc_last == doc_before, jnp.exp(whole), 0.0))
                state = jnp.concatenate([kept, kept], axis=1) * state + fresh
        passed = passed + whole


def scan_kernel(map_ref, prefix_ref):
    rows = map_ref.shape[0] // GROUP
    low = iota((rows, DK), 1) < DK // 2
    state = jnp.zeros((rows, 2 * DV), F32)
    kept = jnp.ones((rows, 2 * DV), F32)
    inside = []
    for chunk in range(GROUP):
        turn = (chunk - lax.axis_index("zh")) & 3
        nth = sum([jnp.where(turn == a, i, 0) for i, a in enumerate(TURN)])
        spans = [pl.ds(node * 16 + nth * 4, 4) for node in range(rows // 4)]
        inside.append((spans, kept, state))
        here = jnp.concatenate([map_ref[span, 0, :] for span in spans], axis=0)
        own = here[:, 2 * DV :]
        other = pltpu.roll(own, DK // 2, 1)
        one, two = jnp.where(low, own, other), jnp.where(low, other, own)
        own = jnp.concatenate([one, one, two, two], axis=1)
        state = own * state + here[:, : 2 * DV]
        kept = own * kept
    row = iota((rows, 2 * DV), 0)
    step = 1
    while step < rows:
        state = kept * jnp.where(row < step, 0.0, pltpu.roll(state, step, 0)) + state
        kept = kept * jnp.where(row < step, 1.0, pltpu.roll(kept, step, 0))
        step *= 2
    before = jnp.where(row < 1, 0.0, pltpu.roll(state, 1, 0))
    for spans, kept, state in inside:
        out = kept * before + state
        for node, span in enumerate(spans):
            prefix_ref[span, 0, :] = out[4 * node : 4 * node + 4]


def finish_kernel(prefix_ref, partial_ref, query_ref, gain_ref, *out_refs):
    state = jnp.concatenate([prefix_ref[:, 0, :DV], prefix_ref[:, 0, DV:]], axis=0)
    head = lax.axis_index("zh")
    gain = gain_ref[pl.ds(head, 1), :]
    for turn, out_ref in enumerate(out_refs):
        span = pl.ds(pl.multiple_of((head ^ turn) * TOK, TOK), TOK)
        mixed = partial_ref[span, :] + dot(query_ref[span, :], state, precision=PRECISE)
        scale = lax.rsqrt(jnp.mean(mixed * mixed, axis=1, keepdims=True) + EPSILON)
        out_ref[...] = (mixed * scale * gain).astype(BF16)


def join_kernel(*refs):
    for turn, ref in enumerate(refs[:-1]):
        head = lax.axis_index("zl") ^ turn
        refs[-1][:, pl.ds(pl.multiple_of(head * DV, DV), DV)] = ref[...]


SMEM = pl.BlockSpec(memory_space=pltpu.SMEM)
VMEM = pl.BlockSpec(memory_space=pltpu.VMEM)
HBM = pl.BlockSpec(memory_space=pltpu.HBM)


def call(kernel, specs, outs, cost=0, scratch=(), limit=32 << 20, out_spec=None):
    return pl.pallas_call(
        kernel,
        out_shape=outs,
        in_specs=specs,
        out_specs=jax.tree.map(lambda _: out_spec or VMEM, outs),
        scratch_shapes=scratch,
        compiler_params=pltpu.CompilerParams(vmem_limit_bytes=limit),
        cost_estimate=pl.CostEstimate(flops=cost, bytes_accessed=1 << 20, transcendentals=0),
    )


def shape(dims, dtype=F32):
    return jax.ShapeDtypeStruct(dims, dtype)


def local(queries, key_vectors, value_vectors, decay_log, assignment, doc_lengths, norm_gain):
    matrix = assignment[0]
    streams = (matrix, queries[0], key_vectors[0], value_vectors[0], decay_log[0])
    packed = call(
        pack_kernel,
        [HBM] * 5,
        shape((4, HEADS, 4, CAP, WIDTH), BF16),
        1 << 28,
        [pltpu.VMEM(a.shape, a.dtype) for a in streams]
        + [pltpu.VMEM((4, HEADS, 4, CAP, WIDTH), BF16)]
        + [pltpu.SemaphoreType.DMA((5,)), pltpu.SemaphoreType.DMA((4,))],
        65500000,
        HBM,
    )(*streams)
    received = lax.all_to_all(packed.reshape(OWNERS, CAP, WIDTH), REGROUP, 0, 0, tiled=True)
    targets, pick = call(
        place_kernel,
        [VMEM],
        (shape((1, OWNERS * CAP), jnp.int32), shape((CHUNK, OWNERS * CAP), BF16)),
        1 << 28,
    )(matrix)
    rows, maps = call(
        maps_kernel,
        [SMEM, VMEM, VMEM],
        (shape((CHUNK, LATE), BF16), shape((OWNERS, 1, 2 * DV + DK))),
        1 << 29,
    )(doc_lengths, pick, received)
    maps = lax.all_to_all(maps, CHUNKS, 0, 0, tiled=True)
    partial, query = call(
        block_kernel,
        [SMEM, VMEM, VMEM, VMEM],
        (shape((CHUNK, DV)), shape((CHUNK, DK))),
        1 << 30,
    )(doc_lengths, targets, received, rows)
    prefix = call(scan_kernel, [VMEM], shape((OWNERS, 1, 2 * DV)), 1 << 24)(maps)
    prefix = lax.all_to_all(prefix, CHUNKS, 0, 0, tiled=True)
    parts = call(finish_kernel, [VMEM] * 4, [shape((TOK, DV), BF16)] * GROUP, 1 << 28)(
        prefix, partial, query, norm_gain.reshape(HEADS, DV)
    )
    pairs = [(head, nth) for head in range(HEADS) for nth in range(GROUP)]
    parts = [
        lax.ppermute(
            part, ("zh", "zl"), [(h * 4 + n, (h + TURN[n]) % 4 * 4 + (h ^ turn)) for h, n in pairs]
        )
        for turn, part in enumerate(parts)
    ]
    out = call(join_kernel, [VMEM] * GROUP, shape((TOK, HEADS * DV), BF16))(*parts)
    return out.reshape(1, TOK, HEADS * DV)


def solution(mesh):
    split = Mesh(mesh.devices.reshape(4, 4, 4, 4, 2), ("y", "zh", "zl", "node", "tp"))
    rows = P("node", CTX, "tp")
    return jax.shard_map(
        local,
        mesh=split,
        in_specs=(rows, rows, rows, rows, P("node", None, None), P(), P("tp")),
        out_specs=rows,
        check_vma=False,
    )
```
